32 devices in a mesh: node: 8 (over z, y), feat: 4 (over x, core).
Axes of the slice: x: 2, y: 2, z: 4, core: 2. Of those that a mesh axis runs over, the one named last changes fastest.
Arguments:
- feature_table: bfloat16 [16384, 768], P('node', 'feat'), may hold values from -6 to 6
- weights: bfloat16 [2, 768, 1024], P(None, 'feat'), may hold values from -0.21875 to 0.21875
- request_rows: int32 [8, 8, 6], P('node'), may hold values from 0 to 2047
- request_counts: int32 [8, 8], P('node'), may hold values from 1 to 6, as said below
- neighbors: int32 [2048, 5], P('node'), may hold values from 0 to 47, as said below
- nbr_counts: int32 [2048], P('node'), may hold values from 1 to 5, as said below
- self_rows: int32 [2048], P('node'), may hold values from 0 to 47, as said below
- grad_hidden: bfloat16 [2048, 1024], P('node'), may hold values from -0.046875 to 0.046875
Outputs:
- hidden: bfloat16 [2048, 1024], P(('node', 'feat'))
- weight_grad: float32 [2, 768, 1024], P(None, 'feat')
The draws below stay inside these ranges and needn't reach their ends.
Inputs may be any that keep to these rules, and one draw needn't show every extreme that they name: `request_counts`: every node index asks each owner for at most 6 rows; in every draw some owner gets exactly 6 from every node index. `neighbors`: each entry is o * 6 + s for an owner o and a slot s below request_counts of the target's node index and o, entries beyond nbr_counts too. `self_rows`: likewise a live slot o * 6 + s of the target's node index. `nbr_counts`: some target of every node index has 5.
All inputs are finite; a program needn't handle non-finite values.
Results may differ from the reference program's by a relative error of at most 0.0033.
Values may be sent and summed in bfloat16 or wider, within the bound.
A program may use at most 64 MiB of HBM per device.

```python
import jax
import jax.numpy as jnp
from jax import lax

F = 768
H = 1024
ROWS_DEV = 2048
TGT_DEV = 256
CAP = 6
FAN = 5
PEERS = 8
ROWS = 16384
TARGETS = 2048


def live_counts(key):
    key_base, key_hot, key_forced = jax.random.split(key, 3)
    regular = jax.random.randint(key_base, (PEERS, PEERS), CAP // 2, CAP + 1)
    heavy = jax.random.randint(key_hot, (PEERS,), 0, 8) == 0
    forced = jax.random.randint(key_forced, (), 0, PEERS)
    heavy = jnp.logical_or(heavy, jnp.arange(PEERS) == forced)
    return jnp.where(heavy[None, :], CAP, regular).astype(jnp.int32)


def live_index(key, counts, width):
    key_owner, key_slot = jax.random.split(key, 2)
    owner = jax.random.randint(key_owner, (TARGETS, width), 0, PEERS)
    spread = jax.random.randint(key_slot, (TARGETS, width), 0, 1048576)
    requester = (jnp.arange(TARGETS, dtype=jnp.int32) // TGT_DEV)[:, None]
    limit = counts[requester, owner]
    return (owner * CAP + spread % limit).astype(jnp.int32)


def draw_request_counts(key, part):
    counts = live_counts(key)
    return counts


def draw_neighbors(key, part):
    counts = live_counts(key)
    key = jax.random.fold_in(key, 5)
    return live_index(key, counts, FAN)


def draw_self_rows(key, part):
    counts = live_counts(key)
    key = jax.random.fold_in(key, 7)
    return live_index(key, counts, 1)[:, 0]


def draw_nbr_counts(key, part):
    key = jax.random.fold_in(key, 9)
    key_count, key_place = jax.random.split(key, 2)
    counts = jax.random.randint(key_count, (TARGETS,), 1, FAN + 1)
    places = jax.random.randint(key_place, (PEERS,), 0, TGT_DEV) + jnp.arange(PEERS) * TGT_DEV
    return counts.at[places].set(FAN).astype(jnp.int32)


def place_ends(entries, key, low, high):
    place = [jax.random.randint(jax.random.fold_in(key, axis), (), 0, length) for axis, length in enumerate(entries.shape)]
    longest = entries.shape.index(max(entries.shape))
    beside = place[:longest] + [(place[longest] + 1) % entries.shape[longest]] + place[longest + 1:]
    return entries.at[tuple(place)].set(low).at[tuple(beside)].set(high)


def levels(rng, extent, cuts, low, high):
    loudness, own = 1.0, jax.random.fold_in(rng, 6)
    for axis_at, parts in cuts:
        draws = jnp.exp(jax.random.uniform(jax.random.fold_in(own, axis_at), (parts,), jnp.float32, low / len(cuts), high / len(cuts)))
        loudness = loudness * jnp.repeat(draws, extent[axis_at] // parts).reshape([-1 if axis == axis_at else 1 for axis in range(len(extent))])
    return loudness


def centred(stream_key, shape, scale, bound, cuts=(), kind=jnp.bfloat16):
    entries = scale * jax.random.normal(stream_key, shape, jnp.float32)
    if cuts:
        entries = entries * levels(stream_key, shape, cuts, -0.22, 0.18)
    return jnp.clip(entries, -bound, bound).astype(kind)


def setup_inputs(seed: int = 0) -> dict:
    key_list = jax.random.split(jax.random.key(seed), 9)
    return {
        "feature_table": centred(key_list[0], (ROWS, F), 1.0, 6.0, ((0, 8), (1, 4))),
        "weights": centred(key_list[1], (2, F, H), F ** -0.5, 0.21875, ((1, 4),)),
        "request_rows": place_ends(jax.random.randint(key_list[2], (PEERS, PEERS, CAP), 0, ROWS_DEV), jax.random.fold_in(key_list[2], 1), 0, ROWS_DEV - 1).astype(jnp.int32),
        "request_counts": draw_request_counts(jax.random.fold_in(key_list[8], 71), 0),
        "neighbors": draw_neighbors(jax.random.fold_in(key_list[8], 71), 0),
        "nbr_counts": draw_nbr_counts(jax.random.fold_in(key_list[8], 71), 0),
        "self_rows": draw_self_rows(jax.random.fold_in(key_list[8], 71), 0),
        "grad_hidden": centred(key_list[7], (TARGETS, H), (2.0 / TGT_DEV), 0.046875, ((0, 8),)),
    }


def smooth_gate(values):
    return 0.5 * values * (1.0 + jnp.tanh(0.7978845608 * (values + 0.044715 * values * values * values)))

def activate(preact, upstream):
    output, pullback = jax.vjp(smooth_gate, preact)
    slope = pullback(upstream.astype(jnp.float32))[0]
    return (output.astype(jnp.bfloat16), slope.astype(jnp.bfloat16))

def aggregate(frontier, local_nbrs, local_counts):
    picked = frontier[local_nbrs]
    within = jnp.arange(local_nbrs.shape[1], dtype=jnp.int32)[None, :] < local_counts[:, None]
    summed = lax.optimization_barrier(jnp.sum(jnp.where(within[:, :, None], picked, jnp.zeros_like(picked)), axis=1, dtype=jnp.float32))
    return (summed / local_counts[:, None].astype(jnp.float32)).astype(jnp.bfloat16)

def reference(feature_table, weights, request_rows, request_counts, neighbors, nbr_counts, self_rows, grad_hidden):
    owner_base = (jnp.arange(PEERS, dtype=jnp.int32) * ROWS_DEV)[:, None]
    slot_index = jnp.arange(CAP, dtype=jnp.int32)[None, :]

    def per_group(running, requester):
        wanted = (owner_base + request_rows[requester]).astype(jnp.int32)
        fetched = feature_table[wanted]
        filled = slot_index < request_counts[requester][:, None]
        frontier = jnp.where(filled[:, :, None], fetched, jnp.zeros_like(fetched)).reshape(PEERS * CAP, F)
        offset = (requester * TGT_DEV).astype(jnp.int32)
        local_nbrs = lax.dynamic_slice_in_dim(neighbors, offset, TGT_DEV, 0)
        local_counts = lax.dynamic_slice_in_dim(nbr_counts, offset, TGT_DEV, 0)
        local_self = lax.dynamic_slice_in_dim(self_rows, offset, TGT_DEV, 0)
        upstream = lax.dynamic_slice_in_dim(grad_hidden, offset, TGT_DEV, 0)
        own_rows = frontier[local_self]
        averaged = aggregate(frontier, local_nbrs, local_counts)
        preact = jnp.dot(own_rows, weights[0], preferred_element_type=jnp.float32) + jnp.dot(averaged, weights[1], preferred_element_type=jnp.float32)
        output, slope = activate(preact, upstream)
        grad_terms = jnp.stack([jnp.dot(own_rows.T, slope, preferred_element_type=jnp.float32), jnp.dot(averaged.T, slope, preferred_element_type=jnp.float32)])
        return (running + grad_terms, output)
    start_sum = jnp.zeros((2, F, H), jnp.float32)
    weight_grad, blocks = lax.scan(per_group, start_sum, jnp.arange(PEERS, dtype=jnp.int32))
    return (blocks.reshape(TARGETS, H), weight_grad)
```

```python
import functools

import jax
import jax.numpy as jnp
from jax import lax
from jax.experimental import pallas as pl
from jax.experimental.pallas import tpu as pltpu
from jax.sharding import PartitionSpec as P

MESH = pl.DeviceIdType.MESH
F32, BF16 = jnp.float32, jnp.bfloat16


def matmul(left, right, exact=False):
    return jnp.dot(
        left,
        right,
        preferred_element_type=F32,
        precision=lax.Precision.HIGHEST if exact else None,
    )


def step_kernel(
    sizes,
    asked_ref,
    counts_ref,
    nbrs_ref,
    nbr_counts_ref,
    self_ref,
    table_ref,
    weights_ref,
    upstream_ref,
    hidden_ref,
    grad_ref,
    table,
    upstream,
    asked,
    looked,
    front,
    proj,
    hid_out,
    hid_in,
    terms,
    grad,
    local_sem,
    ask_send,
    ask_recv,
    look_send,
    look_recv,
    front_send,
    front_recv,
    proj_send,
    proj_recv,
    hid_send,
    hid_recv,
    term_send,
    term_recv,
    out_sem,
):
    nodes, feats, caps, fan = sizes
    slots = nodes * caps
    depth = nodes // 2
    portion = hid_in.shape[1]
    width = hid_in.shape[2]
    me, mine = lax.axis_index("node"), lax.axis_index("feat")
    z, y, x, core = me // 2, me % 2, mine // 2, mine % 2
    node_peers = [lax.rem(me + k, nodes) for k in range(1, nodes)]
    feat_peers = [lax.rem(mine + k, feats) for k in range(1, feats)]
    my_columns = pl.ds(pl.multiple_of(mine * width, width), width)

    def columns(index):
        return pl.ds(pl.multiple_of(index * width, width), width)

    def remote(src, dst, send, recv, node, feat):
        return pltpu.make_async_remote_copy(
            src_ref=src,
            dst_ref=dst,
            send_sem=send,
            recv_sem=recv,
            device_id=(node, feat),
            device_id_type=MESH,
        )

    load_table = pltpu.make_async_copy(table_ref, table, local_sem.at[0])
    load_table.start()
    load_up = pltpu.make_async_copy(upstream_ref.at[:, my_columns], upstream, local_sem.at[1])
    load_up.start()
    load_proj = pltpu.make_async_copy(
        weights_ref.at[:, :, my_columns], proj.at[mine], local_sem.at[2]
    )
    load_proj.start()

    barrier = pltpu.get_barrier_semaphore()
    for peer in node_peers:
        pl.semaphore_signal(barrier, inc=1, device_id=(peer, mine), device_id_type=MESH)
    for peer in feat_peers:
        pl.semaphore_signal(barrier, inc=1, device_id=(me, peer), device_id_type=MESH)

    targets = nbrs_ref.shape[1]
    slot = lax.broadcasted_iota(jnp.int32, (slots, targets), 0)
    owner = jnp.zeros_like(slot)
    for k in range(1, nodes):
        owner = owner + (slot >= k * caps).astype(jnp.int32)
    limit = jnp.zeros_like(slot)
    for k in range(nodes):
        limit = jnp.where(owner == k, counts_ref[0, k], limit)
    live = slot - owner * caps < limit
    chosen = jnp.where(live & (slot == self_ref[...]), 1.0, 0.0).astype(F32)
    valid = nbr_counts_ref[...]
    tally = jnp.zeros((slots, targets), F32)
    for k in range(fan):
        tally = tally + jnp.where((slot == nbrs_ref[k : k + 1, :]) & (valid > k), 1.0, 0.0)
    mean = jnp.where(live, tally / valid.astype(F32), 0.0)
    chosen_rows = chosen.T.astype(BF16)
    mean_rows = mean.T

    pl.semaphore_wait(barrier, nodes + feats - 2)

    sends = []
    for k, peer in enumerate(node_peers):
        copy = remote(asked_ref.at[peer], asked.at[me], ask_send.at[k], ask_recv.at[me], peer, mine)
        copy.start()
        sends.append(copy)
    for k, peer in enumerate(feat_peers):
        copy = remote(
            weights_ref.at[:, :, columns(peer)],
            proj.at[mine],
            proj_send.at[k],
            proj_recv.at[mine],
            me,
            peer,
        )
        copy.start()
        sends.append(copy)
    asked[pl.ds(me, 1)] = asked_ref[pl.ds(me, 1)]
    for peer in node_peers:
        remote(asked.at[peer], asked.at[peer], ask_send.at[0], ask_recv.at[peer], peer, mine).wait_recv()
    wanted = asked[0]
    for k in range(1, nodes):
        wanted = wanted + asked[k]
    load_table.wait()
    rows = table.shape[1]
    pick = (lax.broadcasted_iota(jnp.int32, (rows, wanted.shape[1]), 0) == wanted).astype(F32)
    found = matmul(table[...], pick.astype(BF16)).T
    looked[pl.ds(me, 1)] = found[:slots].astype(BF16)[None]
    for k, peer in enumerate(node_peers):
        copy = remote(looked.at[me], looked.at[me], look_send.at[k], look_recv.at[me], peer, mine)
        copy.start()
        sends.append(copy)
    for peer in node_peers:
        remote(looked.at[peer], looked.at[peer], look_send.at[0], look_recv.at[peer], peer, mine).wait_recv()

    every = looked[...].reshape(nodes * slots, looked.shape[2])

    def order(requester):
        row = lax.broadcasted_iota(jnp.int32, (slots, nodes * slots), 0)
        col = lax.broadcasted_iota(jnp.int32, (slots, nodes * slots), 1)
        block = jnp.zeros_like(row)
        for k in range(1, nodes):
            block = block + (row >= k * caps).astype(jnp.int32)
        place = block * slots + requester * caps + (row - block * caps)
        return (col == place).astype(F32).astype(BF16)

    front[pl.ds(mine, 1)] = matmul(order(me), every).astype(BF16)[None]
    for k, peer in enumerate(feat_peers):
        copy = remote(front.at[mine], front.at[mine], front_send.at[k], front_recv.at[mine], me, peer)
        copy.start()
        sends.append(copy)

    ordered = jnp.concatenate(
        [matmul(order(r), every).astype(BF16) for r in range(nodes)], axis=0
    ).T

    def project(index):
        held = front[pl.ds(index, 1)][0]
        own_rows = matmul(chosen_rows, held).astype(BF16)
        averaged = matmul(mean_rows, held.astype(F32), exact=True).astype(BF16)
        weight = proj[pl.ds(index, 1)][0]
        return matmul(own_rows, weight[0]) + matmul(averaged, weight[1])

    load_proj.wait()
    preact = project(mine)
    for peer in feat_peers:
        remote(front.at[peer], front.at[peer], front_send.at[0], front_recv.at[peer], me, peer).wait_recv()
        remote(proj.at[peer], proj.at[peer], proj_send.at[0], proj_recv.at[peer], me, peer).wait_recv()
        preact = preact + project(peer)

    square = preact * preact
    bent = jnp.tanh(0.7978845608 * (preact + 0.044715 * preact * square))
    rise = 0.7978845608 * (1.0 + 3.0 * 0.044715 * square)
    half = 0.5 * (1.0 + bent)
    load_up.wait()
    slope = upstream[...].astype(F32) * (half + 0.5 * preact * (1.0 - bent * bent) * rise)
    slope = slope.astype(BF16)
    terms[pl.ds(mine, 1), pl.ds(me, 1), 0:1] = (
        matmul(chosen.astype(BF16), slope).astype(BF16)[None, None, None]
    )
    terms[pl.ds(mine, 1), pl.ds(me, 1), 1:2] = (
        matmul(mean, slope.astype(F32), exact=True).astype(BF16)[None, None, None]
    )

    flip_y, flip_x, flip_core = 1 - y, 1 - x, 1 - core
    depths = [z] + [lax.rem(z + k, depth) for k in range(1, depth)]
    counter = [0]

    def pass_on(node, feat, to_node, to_feat):
        copy = remote(
            terms.at[feat, node],
            terms.at[feat, node],
            term_send.at[counter[0]],
            term_recv.at[feat, node],
            to_node,
            to_feat,
        )
        counter[0] += 1
        copy.start()
        sends.append(copy)

    def arrived(node, feat):
        remote(
            terms.at[feat, node],
            terms.at[feat, node],
            term_send.at[0],
            term_recv.at[feat, node],
            me,
            2 * x + flip_core,
        ).wait_recv()

    to_y = (2 * z + flip_y, mine)
    to_x = (me, 2 * flip_x + core)
    to_core = (me, 2 * x + flip_core)
    for k in range(1, depth):
        pass_on(me, mine, 2 * depths[k] + y, mine)
    for k in range(depth):
        node = 2 * depths[k] + y
        if k > 0:
            arrived(node, mine)
        for target in (to_y, to_x, to_core):
            pass_on(node, mine, *target)

    hid_out[...] = (preact * half).astype(BF16)

    def out_rows(index):
        return hid_out.at[pl.ds(pl.multiple_of(index * portion, portion), portion), :]

    for k, peer in enumerate(feat_peers):
        copy = remote(out_rows(peer), hid_in.at[mine], hid_send.at[k], hid_recv.at[mine], me, peer)
        copy.start()
        sends.append(copy)
    hid_in[pl.ds(mine, 1)] = hid_out[pl.ds(pl.multiple_of(mine * portion, portion), portion), :][None]

    across = 2 * flip_x + core
    early = depth // 2
    for k in range(depth):
        node_y, node_x = 2 * depths[k] + flip_y, 2 * depths[k] + y
        arrived(node_y, mine)
        if k < early:
            pass_on(node_y, mine, *to_x)
        arrived(node_x, across)
        if k >= early:
            pass_on(node_x, across, *to_y)
        pass_on(node_y, mine, *to_core)
        pass_on(node_x, across, *to_core)

    outs = []

    def gradient(feat, at):
        held = terms[pl.ds(feat, 1)][0]
        for layer in range(2):
            part = held[:, layer].reshape(nodes * slots, width)
            grad[at, layer] = matmul(ordered, part)
        copy = pltpu.make_async_copy(
            grad.at[at], grad_ref.at[:, :, columns(feat)], out_sem.at[at]
        )
        copy.start()
        outs.append(copy)

    gradient(mine, 0)
    for k in range(depth):
        node = 2 * depths[k] + flip_y
        arrived(node, across)
        pass_on(node, across, *to_core)
    gradient(across, 1)
    for at, feat in ((2, 2 * x + flip_core), (3, 2 * flip_x + flip_core)):
        for node in range(nodes):
            arrived(node, feat)
        gradient(feat, at)

    for peer in feat_peers:
        remote(hid_in.at[peer], hid_in.at[peer], hid_send.at[0], hid_recv.at[peer], me, peer).wait_recv()
    for k in range(feats):
        hidden_ref[:, k * width : (k + 1) * width] = hid_in[k]
    for copy in sends:
        copy.wait_send()
    for copy in outs:
        copy.wait()


def compact_step(
    feature_table,
    weights,
    request_rows,
    request_counts,
    neighbors,
    nbr_counts,
    self_rows,
    grad_hidden,
):
    nodes, feats = lax.axis_size("node"), lax.axis_size("feat")
    caps, fan = request_rows.shape[2], neighbors.shape[1]
    slots = nodes * caps
    targets, hidden = grad_hidden.shape
    rows, features = feature_table.shape
    width, portion = hidden // feats, targets // feats
    me = lax.axis_index("node")
    lane = jnp.arange(128, dtype=jnp.int32)
    spread = jnp.pad(jnp.tile(request_rows[0], (1, nodes)), ((0, 0), (0, 128 - slots)))
    asked = jnp.where(lane[None, :] // caps == me, spread, 0).reshape(nodes, 1, 128)
    dma = pltpu.SemaphoreType.DMA
    vmem = pl.BlockSpec(memory_space=pltpu.VMEM)
    anywhere = pl.BlockSpec(memory_space=pl.ANY)
    moves = 2 * nodes * feats
    return pl.pallas_call(
        functools.partial(step_kernel, (nodes, feats, caps, fan)),
        out_shape=(
            jax.ShapeDtypeStruct((portion, hidden), BF16),
            jax.ShapeDtypeStruct((2, features, hidden), F32),
        ),
        in_specs=[
            vmem,
            pl.BlockSpec(memory_space=pltpu.SMEM),
            vmem,
            vmem,
            vmem,
            anywhere,
            anywhere,
            anywhere,
        ],
        out_specs=(vmem, anywhere),
        scratch_shapes=[
            pltpu.VMEM((features, rows), BF16),
            pltpu.VMEM((targets, width), BF16),
            pltpu.VMEM((nodes, 1, 128), jnp.int32),
            pltpu.VMEM((nodes, slots, features), BF16),
            pltpu.VMEM((feats, slots, features), BF16),
            pltpu.VMEM((feats, 2, features, width), BF16),
            pltpu.VMEM((targets, width), BF16),
            pltpu.VMEM((feats, portion, width), BF16),
            pltpu.VMEM((feats, nodes, 2, slots, width), BF16),
            pltpu.VMEM((feats, 2, features, width), F32),
            dma((3,)),
            dma((nodes,)),
            dma((nodes,)),
            dma((nodes,)),
            dma((nodes,)),
            dma((feats,)),
            dma((feats,)),
            dma((feats,)),
            dma((feats,)),
            dma((feats,)),
            dma((feats,)),
            dma((moves,)),
            dma((feats, nodes)),
            dma((feats,)),
        ],
        compiler_params=pltpu.CompilerParams(
            collective_id=0, has_side_effects=True, vmem_limit_bytes=32 * 1024 * 1024
        ),
    )(
        asked,
        request_counts,
        neighbors.T,
        nbr_counts[None],
        self_rows[None],
        feature_table.T,
        weights,
        grad_hidden,
    )


def smooth_gate(values):
    return (
        0.5
        * values
        * (1.0 + jnp.tanh(0.7978845608 * (values + 0.044715 * values * values * values)))
    )


def activate(preact, upstream):
    output, pullback = jax.vjp(smooth_gate, preact)
    slope = pullback(upstream.astype(jnp.float32))[0]
    return (output.astype(jnp.bfloat16), slope.astype(jnp.bfloat16))


def aggregate(frontier, local_nbrs, local_counts):
    picked = frontier[local_nbrs]
    within = jnp.arange(local_nbrs.shape[1], dtype=jnp.int32)[None, :] < local_counts[:, None]
    summed = jnp.sum(
        jnp.where(within[:, :, None], picked, jnp.zeros_like(picked)), axis=1, dtype=jnp.float32
    )
    return (summed / local_counts[:, None].astype(jnp.float32)).astype(jnp.bfloat16)


def project(own_rows, averaged, weights):
    first = jnp.dot(own_rows, weights[0], preferred_element_type=jnp.float32)
    return first + jnp.dot(averaged, weights[1], preferred_element_type=jnp.float32)


def contract(left_side, right_side):
    return lax.dot_general(
        left_side, right_side, (((0,), (0,)), ((), ())), preferred_element_type=jnp.float32
    )


def per_device(
    feature_table,
    weights,
    request_rows,
    request_counts,
    neighbors,
    nbr_counts,
    self_rows,
    grad_hidden,
):
    slot_count = request_rows.shape[2]
    looked = feature_table[
        lax.all_to_all(request_rows[0], "node", split_axis=0, concat_axis=0, tiled=True)
    ]
    fetched = lax.all_to_all(looked, "node", split_axis=0, concat_axis=0, tiled=True)
    filled = jnp.arange(slot_count, dtype=jnp.int32)[None, :] < request_counts[0][:, None]
    frontier = jnp.where(filled[:, :, None], fetched, jnp.zeros_like(fetched)).reshape(
        -1, fetched.shape[2]
    )
    own_rows = frontier[self_rows]
    averaged = aggregate(frontier, neighbors, nbr_counts)
    groups = lax.axis_size("feat")
    portion = own_rows.shape[0] // groups
    preact = lax.psum(project(own_rows, averaged, weights), "feat")
    output_all, slope = activate(preact, grad_hidden)
    hidden = lax.dynamic_slice_in_dim(output_all, lax.axis_index("feat") * portion, portion, 0)
    grad_terms = jnp.stack([contract(own_rows, slope), contract(averaged, slope)])
    weight_grad = lax.psum(grad_terms, "node")
    return (hidden, weight_grad)


def solution(mesh):
    placed = (
        P("node", "feat"),
        P(None, "feat", None),
        P("node", None, None),
        P("node", None),
        P("node", None),
        P("node"),
        P("node"),
        P("node", None),
    )
    nodes, feats = mesh.shape["node"], mesh.shape["feat"]

    def per_slice(feature_table, weights, request_rows, *others):
        slots = nodes * request_rows.shape[2]
        plan = per_device
        if feats == 4 and nodes % 2 == 0 and slots % 16 == 0 and slots <= 128:
            plan = compact_step
        return plan(feature_table, weights, request_rows, *others)

    return jax.shard_map(
        per_slice,
        mesh=mesh,
        in_specs=placed,
        out_specs=(P(("node", "feat"), None), P(None, "feat", None)),
        check_vma=False,
    )
```

```python
import functools

import jax
import jax.numpy as jnp
from jax import lax
from jax.experimental import pallas as pl
from jax.experimental.pallas import tpu as pltpu
from jax.sharding import PartitionSpec as P

MESH = pl.DeviceIdType.MESH
F32, BF16 = jnp.float32, jnp.bfloat16


def matmul(left, right):
    return jnp.dot(left, right, preferred_element_type=F32)


def step_kernel(
    sizes,
    request_ref,
    counts_ref,
    nbrs_ref,
    nbr_counts_ref,
    self_ref,
    table_ref,
    weights_ref,
    upstream_ref,
    hidden_ref,
    terms,
    ordered_ref,
    request,
    counts,
    nbrs,
    nbr_counts,
    self_rows,
    table,
    upstream,
    ask_out,
    asked,
    stacked,
    looked,
    front,
    proj,
    preact_ref,
    hid_out,
    own_terms,
    in_order,
    local_sem,
    ask_send,
    ask_recv,
    look_send,
    look_recv,
    front_send,
    front_recv,
    proj_send,
    proj_recv,
    hid_send,
    hid_recv,
    term_send,
    term_recv,
):
    nodes, feats, caps, fan = sizes
    slots = nodes * caps
    depth = nodes // 2
    portion = hidden_ref.shape[1]
    width = hidden_ref.shape[2]
    me, mine = lax.axis_index("node"), lax.axis_index("feat")
    z, y, x, core = me // 2, me % 2, mine // 2, mine % 2
    node_peers = [lax.rem(me + k, nodes) for k in range(1, nodes)]
    feat_peers = [lax.rem(mine + k, feats) for k in range(1, feats)]
    my_columns = pl.ds(pl.multiple_of(mine * width, width), width)

    def columns(index):
        return pl.ds(pl.multiple_of(index * width, width), width)

    def remote(src, dst, send, recv, node, feat):
        return pltpu.make_async_remote_copy(
            src_ref=src,
            dst_ref=dst,
            send_sem=send,
            recv_sem=recv,
            device_id=(node, feat),
            device_id_type=MESH,
        )

    loads = []
    for k, (src, dst) in enumerate(
        (
            (request_ref, request),
            (nbrs_ref, nbrs),
            (nbr_counts_ref, nbr_counts),
            (self_ref, self_rows),
            (counts_ref, counts),
            (table_ref, table),
            (weights_ref.at[:, :, my_columns], proj.at[mine]),
            (upstream_ref.at[:, my_columns], upstream),
        )
    ):
        copy = pltpu.make_async_copy(src, dst, local_sem.at[k])
        copy.start()
        loads.append(copy)

    barrier = pltpu.get_barrier_semaphore()
    for peer in node_peers:
        pl.semaphore_signal(barrier, inc=1, device_id=(peer, mine), device_id_type=MESH)
    for peer in feat_peers:
        pl.semaphore_signal(barrier, inc=1, device_id=(me, peer), device_id_type=MESH)

    ask_out[...] = jnp.zeros_like(ask_out)
    loads[0].wait()
    for k in range(caps):
        ask_out[k : k + 1, 0:nodes] = request[k]
    pl.semaphore_wait(barrier, nodes + feats - 2)

    sends = []
    for k, peer in enumerate(node_peers):
        copy = remote(ask_out, asked.at[me], ask_send.at[k], ask_recv.at[me], peer, mine)
        copy.start()
        sends.append(copy)
    for k, peer in enumerate(feat_peers):
        copy = remote(
            weights_ref.at[:, :, columns(peer)],
            proj.at[mine],
            proj_send.at[k],
            proj_recv.at[mine],
            me,
            peer,
        )
        copy.start()
        sends.append(copy)
    asked[pl.ds(me, 1)] = ask_out[...][None]

    for copy in loads[1:5]:
        copy.wait()
    targets = nbrs.shape[1]

    def owner_of(slot):
        owner = jnp.zeros_like(slot)
        for k in range(1, nodes):
            owner = owner + (slot >= k * caps).astype(jnp.int32)
        return owner

    held_by = owner_of(lax.broadcasted_iota(jnp.int32, (slots, nodes), 0))
    here = lax.broadcasted_iota(jnp.int32, (slots, nodes), 1) == held_by
    limit = jnp.sum(
        jnp.where(here, counts[...].astype(F32), 0.0), axis=1, keepdims=True
    )
    slot = lax.broadcasted_iota(jnp.int32, (slots, targets), 0)
    live = (slot - owner_of(slot) * caps).astype(F32) < limit
    chosen = jnp.where(live & (slot == self_rows[...]), 1.0, 0.0).astype(F32)
    valid = nbr_counts[...]
    tally = jnp.zeros((slots, targets), F32)
    for k in range(fan):
        tally = tally + jnp.where((slot == nbrs[k : k + 1, :]) & (valid > k), 1.0, 0.0)
    tally = jnp.where(live, tally, 0.0)
    share = 1.0 / valid.astype(F32)
    mean = tally * share
    mean_high = mean.astype(BF16)
    mean_low = (mean - mean_high.astype(F32)).astype(BF16)
    back = jnp.concatenate([chosen.astype(BF16), mean_high, mean_low], axis=0)
    chosen_rows = chosen.T.astype(BF16)
    tally_rows = tally.T.astype(BF16)
    share_rows = jnp.broadcast_to(share, (128, targets)).T[:, 0:1]

    for peer in node_peers:
        remote(asked.at[peer], asked.at[peer], ask_send.at[0], ask_recv.at[peer], peer, mine).wait_recv()
    for r in range(nodes):
        stacked[r * caps : (r + 1) * caps, :] = asked[r, 0:caps, :]
    lane = lax.broadcasted_iota(jnp.int32, stacked.shape, 1)
    wanted = jnp.sum(
        jnp.where(lane == me, stacked[...].astype(F32), 0.0), axis=1, keepdims=True
    ).astype(jnp.int32)
    rows = table.shape[1]
    pick = (lax.broadcasted_iota(jnp.int32, (slots, rows), 1) == wanted).astype(F32)
    loads[5].wait()
    found = lax.dot_general(
        pick.astype(BF16), table[...], (((1,), (1,)), ((), ())), preferred_element_type=F32
    )
    looked[pl.ds(me, 1)] = found.astype(BF16)[None]
    for k, peer in enumerate(node_peers):
        copy = remote(looked.at[me], looked.at[me], look_send.at[k], look_recv.at[me], peer, mine)
        copy.start()
        sends.append(copy)
    for peer in node_peers:
        remote(looked.at[peer], looked.at[peer], look_send.at[0], look_recv.at[peer], peer, mine).wait_recv()

    every = looked[...].reshape(nodes * slots, looked.shape[2])

    def order(requester):
        row = lax.broadcasted_iota(jnp.int32, (slots, nodes * slots), 0)
        col = lax.broadcasted_iota(jnp.int32, (slots, nodes * slots), 1)
        block = owner_of(row)
        place = block * slots + requester * caps + (row - block * caps)
        return (col == place).astype(F32).astype(BF16)

    front[pl.ds(mine, 1)] = matmul(order(me), every).astype(BF16)[None]
    for k, peer in enumerate(feat_peers):
        copy = remote(front.at[mine], front.at[mine], front_send.at[k], front_recv.at[mine], me, peer)
        copy.start()
        sends.append(copy)

    @pl.loop(0, nodes)
    def _(r):
        start = pl.multiple_of(r * slots, slots)
        in_order[pl.ds(start, slots), :] = matmul(order(r), every).astype(BF16)

    ordered_ref[...] = in_order[...].T

    loads[6].wait()
    preact_ref[...] = jnp.zeros_like(preact_ref)

    @pl.loop(0, feats)
    def _(k):
        index = lax.rem(mine + k, feats)

        @pl.when(k > 0)
        def _():
            remote(front.at[index], front.at[index], front_send.at[0], front_recv.at[index], me, index).wait_recv()
            remote(proj.at[index], proj.at[index], proj_send.at[0], proj_recv.at[index], me, index).wait_recv()

        held = front[pl.ds(index, 1)][0]
        own_rows = matmul(chosen_rows, held).astype(BF16)
        averaged = (matmul(tally_rows, held) * share_rows).astype(BF16)
        weight = proj[pl.ds(index, 1)][0]
        preact_ref[...] += matmul(own_rows, weight[0]) + matmul(averaged, weight[1])

    preact = preact_ref[...]
    square = preact * preact
    bent = jnp.tanh(0.7978845608 * (preact + 0.044715 * preact * square))
    rise = 0.7978845608 * (1.0 + 3.0 * 0.044715 * square)
    half = 0.5 * (1.0 + bent)
    loads[7].wait()
    slope = upstream[...].astype(F32) * (half + 0.5 * preact * (1.0 - bent * bent) * rise)
    both = matmul(back, slope.astype(BF16))
    own_terms[0] = both[:slots].astype(BF16)
    own_terms[1] = (both[slots : 2 * slots] + both[2 * slots :]).astype(BF16)
    keep = pltpu.make_async_copy(own_terms, terms.at[mine, me], local_sem.at[8])
    keep.start()

    flip_y, flip_x, flip_core = 1 - y, 1 - x, 1 - core
    depths = [z] + [lax.rem(z + k, depth) for k in range(1, depth)]
    counter = [0]

    def pass_on(node, feat, to_node, to_feat, src=None):
        copy = remote(
            terms.at[feat, node] if src is None else src,
            terms.at[feat, node],
            term_send.at[counter[0]],
            term_recv.at[feat, node],
            to_node,
            to_feat,
        )
        counter[0] += 1
        copy.start()
        sends.append(copy)

    def arrived(node, feat):
        remote(
            terms.at[feat, node],
            terms.at[feat, node],
            term_send.at[0],
            term_recv.at[feat, node],
            me,
            2 * x + flip_core,
        ).wait_recv()

    to_y = (2 * z + flip_y, mine)
    to_x = (me, 2 * flip_x + core)
    to_core = (me, 2 * x + flip_core)
    for k in range(1, depth):
        pass_on(me, mine, 2 * depths[k] + y, mine, own_terms)
    for k in range(depth):
        node = 2 * depths[k] + y
        if k > 0:
            arrived(node, mine)
        for target in (to_y, to_x, to_core):
            pass_on(node, mine, *target, src=own_terms if k == 0 else None)

    hid_out[...] = (preact * half).astype(BF16)

    def out_rows(index):
        return hid_out.at[pl.ds(pl.multiple_of(index * portion, portion), portion), :]

    for k, peer in enumerate(feat_peers):
        copy = remote(out_rows(peer), hidden_ref.at[mine], hid_send.at[k], hid_recv.at[mine], me, peer)
        copy.start()
        sends.append(copy)
    keep_rows = pltpu.make_async_copy(out_rows(mine), hidden_ref.at[mine], local_sem.at[9])
    keep_rows.start()

    across = 2 * flip_x + core
    early = depth // 2
    for k in range(depth):
        node_y, node_x = 2 * depths[k] + flip_y, 2 * depths[k] + y
        arrived(node_y, mine)
        if k < early:
            pass_on(node_y, mine, *to_x)
        arrived(node_x, across)
        if k >= early:
            pass_on(node_x, across, *to_y)
        pass_on(node_y, mine, *to_core)
        pass_on(node_x, across, *to_core)

    for k in range(depth):
        node = 2 * depths[k] + flip_y
        arrived(node, across)
        pass_on(node, across, *to_core)
    for feat in (2 * x + flip_core, 2 * flip_x + flip_core):
        for node in range(nodes):
            arrived(node, feat)
    for peer in feat_peers:
        remote(hidden_ref.at[peer], hidden_ref.at[peer], hid_send.at[0], hid_recv.at[peer], me, peer).wait_recv()
    for copy in sends:
        copy.wait_send()
    keep.wait()
    keep_rows.wait()


def gradient_kernel(hidden_in, terms, ordered, hidden_ref, grad_ref, rows_out, grad, out_sem):
    feats, nodes, layers, slots, width = terms.shape
    for k in range(feats):
        rows_out[:, k * width : (k + 1) * width] = hidden_in[k]
    keep_rows = pltpu.make_async_copy(rows_out, hidden_ref, out_sem.at[feats])
    keep_rows.start()

    def part(feat):
        columns = pl.ds(pl.multiple_of(feat * width, width), width)
        return pltpu.make_async_copy(grad.at[feat], grad_ref.at[:, :, columns], out_sem.at[feat])

    @pl.loop(0, feats)
    def _(feat):
        held = terms[pl.ds(feat, 1)][0]
        for layer in range(layers):
            total = matmul(ordered[...], held[:, layer].reshape(nodes * slots, width))
            grad[pl.ds(feat, 1), layer : layer + 1] = total[None, None]
        part(feat).start()

    @pl.loop(0, feats)
    def _(feat):
        part(feat).wait()

    keep_rows.wait()


def compact_step(
    feature_table,
    weights,
    request_rows,
    request_counts,
    neighbors,
    nbr_counts,
    self_rows,
    grad_hidden,
):
    nodes, feats = lax.axis_size("node"), lax.axis_size("feat")
    caps, fan = request_rows.shape[2], neighbors.shape[1]
    slots = nodes * caps
    targets, hidden = grad_hidden.shape
    rows, features = feature_table.shape
    width, portion = hidden // feats, targets // feats
    dma = pltpu.SemaphoreType.DMA
    vmem = pl.BlockSpec(memory_space=pltpu.VMEM)
    anywhere = pl.BlockSpec(memory_space=pl.ANY)
    moves = nodes * feats - 1
    hidden_in, terms, ordered = pl.pallas_call(
        functools.partial(step_kernel, (nodes, feats, caps, fan)),
        out_shape=(
            jax.ShapeDtypeStruct((feats, portion, width), BF16),
            jax.ShapeDtypeStruct((feats, nodes, 2, slots, width), BF16),
            jax.ShapeDtypeStruct((features, nodes * slots), BF16),
        ),
        in_specs=[pl.BlockSpec(memory_space=pltpu.HBM)] * 8,
        out_specs=(anywhere, anywhere, vmem),
        scratch_shapes=[
            pltpu.VMEM((caps, 1, nodes), jnp.int32),
            pltpu.VMEM((1, nodes), jnp.int32),
            pltpu.VMEM((fan, targets), jnp.int32),
            pltpu.VMEM((1, targets), jnp.int32),
            pltpu.VMEM((1, targets), jnp.int32),
            pltpu.VMEM((features, rows), BF16),
            pltpu.VMEM((targets, width), BF16),
            pltpu.VMEM((8, 128), jnp.int32),
            pltpu.VMEM((nodes, 8, 128), jnp.int32),
            pltpu.VMEM((slots, 128), jnp.int32),
            pltpu.VMEM((nodes, slots, features), BF16),
            pltpu.VMEM((feats, slots, features), BF16),
            pltpu.VMEM((feats, 2, features, width), BF16),
            pltpu.VMEM((targets, width), F32),
            pltpu.VMEM((targets, width), BF16),
            pltpu.VMEM((2, slots, width), BF16),
            pltpu.VMEM((nodes * slots, features), BF16),
            dma((10,)),
            dma((nodes,)),
            dma((nodes,)),
            dma((nodes,)),
            dma((nodes,)),
            dma((feats,)),
            dma((feats,)),
            dma((feats,)),
            dma((feats,)),
            dma((feats,)),
            dma((feats,)),
            dma((moves,)),
            dma((feats, nodes)),
        ],
        compiler_params=pltpu.CompilerParams(
            collective_id=0, has_side_effects=True, vmem_limit_bytes=24 * 1024 * 1024
        ),
    )(
        request_rows.transpose(2, 0, 1),
        request_counts,
        neighbors.T,
        nbr_counts[None],
        self_rows[None],
        feature_table.T,
        weights,
        grad_hidden,
    )
    hbm = pl.BlockSpec(memory_space=pltpu.HBM)
    return pl.pallas_call(
        gradient_kernel,
        out_shape=(
            jax.ShapeDtypeStruct((portion, hidden), BF16),
            jax.ShapeDtypeStruct((2, features, hidden), F32),
        ),
        in_specs=[vmem, vmem, vmem],
        out_specs=(hbm, hbm),
        scratch_shapes=[
            pltpu.VMEM((portion, hidden), BF16),
            pltpu.VMEM((feats, 2, features, width), F32),
            dma((feats + 1,)),
        ],
        compiler_params=pltpu.CompilerParams(vmem_limit_bytes=24 * 1024 * 1024),
    )(hidden_in, terms, ordered)


def smooth_gate(values):
    return (
        0.5
        * values
        * (1.0 + jnp.tanh(0.7978845608 * (values + 0.044715 * values * values * values)))
    )


def activate(preact, upstream):
    output, pullback = jax.vjp(smooth_gate, preact)
    slope = pullback(upstream.astype(jnp.float32))[0]
    return (output.astype(jnp.bfloat16), slope.astype(jnp.bfloat16))


def aggregate(frontier, local_nbrs, local_counts):
    picked = frontier[local_nbrs]
    within = jnp.arange(local_nbrs.shape[1], dtype=jnp.int32)[None, :] < local_counts[:, None]
    summed = jnp.sum(
        jnp.where(within[:, :, None], picked, jnp.zeros_like(picked)), axis=1, dtype=jnp.float32
    )
    return (summed / local_counts[:, None].astype(jnp.float32)).astype(jnp.bfloat16)


def project(own_rows, averaged, weights):
    first = jnp.dot(own_rows, weights[0], preferred_element_type=jnp.float32)
    return first + jnp.dot(averaged, weights[1], preferred_element_type=jnp.float32)


def contract(left_side, right_side):
    return lax.dot_general(
        left_side, right_side, (((0,), (0,)), ((), ())), preferred_element_type=jnp.float32
    )


def per_device(
    feature_table,
    weights,
    request_rows,
    request_counts,
    neighbors,
    nbr_counts,
    self_rows,
    grad_hidden,
):
    slot_count = request_rows.shape[2]
    looked = feature_table[
        lax.all_to_all(request_rows[0], "node", split_axis=0, concat_axis=0, tiled=True)
    ]
    fetched = lax.all_to_all(looked, "node", split_axis=0, concat_axis=0, tiled=True)
    filled = jnp.arange(slot_count, dtype=jnp.int32)[None, :] < request_counts[0][:, None]
    frontier = jnp.where(filled[:, :, None], fetched, jnp.zeros_like(fetched)).reshape(
        -1, fetched.shape[2]
    )
    own_rows = frontier[self_rows]
    averaged = aggregate(frontier, neighbors, nbr_counts)
    groups = lax.axis_size("feat")
    portion = own_rows.shape[0] // groups
    preact = lax.psum(project(own_rows, averaged, weights), "feat")
    output_all, slope = activate(preact, grad_hidden)
    hidden = lax.dynamic_slice_in_dim(output_all, lax.axis_index("feat") * portion, portion, 0)
    grad_terms = jnp.stack([contract(own_rows, slope), contract(averaged, slope)])
    weight_grad = lax.psum(grad_terms, "node")
    return (hidden, weight_grad)


def solution(mesh):
    placed = (
        P("node", "feat"),
        P(None, "feat", None),
        P("node", None, None),
        P("node", None),
        P("node", None),
        P("node"),
        P("node"),
        P("node", None),
    )
    nodes, feats = mesh.shape["node"], mesh.shape["feat"]

    def per_slice(feature_table, weights, request_rows, *others):
        slots = nodes * request_rows.shape[2]
        plan = per_device
        if feats == 4 and nodes % 2 == 0 and slots % 16 == 0 and slots <= 128 and request_rows.shape[2] <= 8:
            plan = compact_step
        return plan(feature_table, weights, request_rows, *others)

    return jax.shard_map(
        per_slice,
        mesh=mesh,
        in_specs=placed,
        out_specs=(P(("node", "feat"), None), P(None, "feat", None)),
        check_vma=False,
    )
```

```python
import functools

import jax
import jax.numpy as jnp
from jax import lax
from jax.experimental import pallas as pl
from jax.experimental.pallas import tpu as pltpu
from jax.sharding import PartitionSpec as P

MESH = pl.DeviceIdType.MESH
F32, BF16 = jnp.float32, jnp.bfloat16


def matmul(left, right):
    return jnp.dot(left, right, preferred_element_type=F32)


def step_kernel(
    sizes,
    request_ref,
    counts_ref,
    nbrs_ref,
    nbr_counts_ref,
    self_ref,
    table_ref,
    weights_ref,
    upstream_ref,
    hidden_ref,
    terms,
    ordered_ref,
    request,
    counts,
    nbrs,
    nbr_counts,
    self_rows,
    table,
    upstream,
    ask_out,
    asked,
    stacked,
    looked,
    front,
    proj,
    preact_ref,
    hid_out,
    own_terms,
    in_order,
    local_sem,
    ask_send,
    ask_recv,
    look_send,
    look_recv,
    front_send,
    front_recv,
    proj_send,
    proj_recv,
    hid_send,
    hid_recv,
    term_send,
    term_recv,
):
    nodes, feats, caps, fan = sizes
    slots = nodes * caps
    depth = nodes // 2
    portion = hidden_ref.shape[1]
    width = hidden_ref.shape[2]
    me, mine = lax.axis_index("node"), lax.axis_index("feat")
    z, y, x, core = me // 2, me % 2, mine // 2, mine % 2
    node_peers = [lax.rem(me + k, nodes) for k in range(1, nodes)]
    feat_peers = [lax.rem(mine + k, feats) for k in range(1, feats)]
    my_columns = pl.ds(pl.multiple_of(mine * width, width), width)

    def columns(index):
        return pl.ds(pl.multiple_of(index * width, width), width)

    def remote(src, dst, send, recv, node, feat):
        return pltpu.make_async_remote_copy(
            src_ref=src,
            dst_ref=dst,
            send_sem=send,
            recv_sem=recv,
            device_id=(node, feat),
            device_id_type=MESH,
        )

    loads = []
    for k, (src, dst) in enumerate(
        (
            (request_ref, request),
            (nbrs_ref, nbrs),
            (nbr_counts_ref, nbr_counts),
            (self_ref, self_rows),
            (counts_ref, counts),
            (table_ref, table),
            (weights_ref.at[:, :, my_columns], proj.at[mine]),
            (upstream_ref.at[:, my_columns], upstream),
        )
    ):
        copy = pltpu.make_async_copy(src, dst, local_sem.at[k])
        copy.start()
        loads.append(copy)

    barrier = pltpu.get_barrier_semaphore()
    for peer in node_peers:
        pl.semaphore_signal(barrier, inc=1, device_id=(peer, mine), device_id_type=MESH)
    for peer in feat_peers:
        pl.semaphore_signal(barrier, inc=1, device_id=(me, peer), device_id_type=MESH)

    ask_out[...] = jnp.zeros_like(ask_out)
    loads[0].wait()
    for k in range(caps):
        ask_out[k : k + 1, 0:nodes] = request[k]
    pl.semaphore_wait(barrier, nodes + feats - 2)

    sends = []
    for k, peer in enumerate(node_peers):
        copy = remote(ask_out, asked.at[me], ask_send.at[k], ask_recv.at[me], peer, mine)
        copy.start()
        sends.append(copy)
    for k, peer in enumerate(feat_peers):
        copy = remote(
            weights_ref.at[:, :, columns(peer)],
            proj.at[mine],
            proj_send.at[k],
            proj_recv.at[mine],
            me,
            peer,
        )
        copy.start()
        sends.append(copy)
    asked[pl.ds(me, 1)] = ask_out[...][None]

    for copy in loads[1:5]:
        copy.wait()
    targets = nbrs.shape[1]

    def owner_of(slot):
        owner = jnp.zeros_like(slot)
        for k in range(1, nodes):
            owner = owner + (slot >= k * caps).astype(jnp.int32)
        return owner

    held_by = owner_of(lax.broadcasted_iota(jnp.int32, (slots, nodes), 0))
    here = lax.broadcasted_iota(jnp.int32, (slots, nodes), 1) == held_by
    limit = jnp.sum(
        jnp.where(here, counts[...].astype(F32), 0.0), axis=1, keepdims=True
    )
    slot = lax.broadcasted_iota(jnp.int32, (slots, targets), 0)
    live = (slot - owner_of(slot) * caps).astype(F32) < limit
    chosen = jnp.where(live & (slot == self_rows[...]), 1.0, 0.0).astype(F32)
    valid = nbr_counts[...]
    tally = jnp.zeros((slots, targets), F32)
    for k in range(fan):
        tally = tally + jnp.where((slot == nbrs[k : k + 1, :]) & (valid > k), 1.0, 0.0)
    tally = jnp.where(live, tally, 0.0)
    share = 1.0 / valid.astype(F32)
    mean = tally * share
    mean_high = mean.astype(BF16)
    mean_low = (mean - mean_high.astype(F32)).astype(BF16)
    back = jnp.concatenate([chosen.astype(BF16), mean_high, mean_low], axis=0)
    chosen_rows = chosen.T.astype(BF16)
    tally_rows = tally.T.astype(BF16)
    share_rows = jnp.broadcast_to(share, (128, targets)).T[:, 0:1]

    for peer in node_peers:
        remote(asked.at[peer], asked.at[peer], ask_send.at[0], ask_recv.at[peer], peer, mine).wait_recv()
    for r in range(nodes):
        stacked[r * caps : (r + 1) * caps, :] = asked[r, 0:caps, :]
    lane = lax.broadcasted_iota(jnp.int32, stacked.shape, 1)
    wanted = jnp.sum(
        jnp.where(lane == me, stacked[...].astype(F32), 0.0), axis=1, keepdims=True
    ).astype(jnp.int32)
    rows = table.shape[1]
    pick = (lax.broadcasted_iota(jnp.int32, (slots, rows), 1) == wanted).astype(F32)
    loads[5].wait()
    found = lax.dot_general(
        pick.astype(BF16), table[...], (((1,), (1,)), ((), ())), preferred_element_type=F32
    )
    looked[pl.ds(me, 1)] = found.astype(BF16)[None]
    for k, peer in enumerate(node_peers):
        copy = remote(looked.at[me], looked.at[me], look_send.at[k], look_recv.at[me], peer, mine)
        copy.start()
        sends.append(copy)
    for peer in node_peers:
        remote(looked.at[peer], looked.at[peer], look_send.at[0], look_recv.at[peer], peer, mine).wait_recv()

    every = looked[...].reshape(nodes * slots, looked.shape[2])

    def order(requester):
        row = lax.broadcasted_iota(jnp.int32, (slots, nodes * slots), 0)
        col = lax.broadcasted_iota(jnp.int32, (slots, nodes * slots), 1)
        block = owner_of(row)
        place = block * slots + requester * caps + (row - block * caps)
        return (col == place).astype(F32).astype(BF16)

    front[pl.ds(mine, 1)] = matmul(order(me), every).astype(BF16)[None]
    for k, peer in enumerate(feat_peers):
        copy = remote(front.at[mine], front.at[mine], front_send.at[k], front_recv.at[mine], me, peer)
        copy.start()
        sends.append(copy)

    @pl.loop(0, nodes)
    def _(r):
        start = pl.multiple_of(r * slots, slots)
        in_order[pl.ds(start, slots), :] = matmul(order(r), every).astype(BF16)

    ordered_ref[...] = in_order[...].T

    loads[6].wait()
    preact_ref[...] = jnp.zeros_like(preact_ref)

    @pl.loop(0, feats)
    def _(k):
        index = lax.rem(mine + k, feats)

        @pl.when(k > 0)
        def _():
            remote(front.at[index], front.at[index], front_send.at[0], front_recv.at[index], me, index).wait_recv()
            remote(proj.at[index], proj.at[index], proj_send.at[0], proj_recv.at[index], me, index).wait_recv()

        held = front[pl.ds(index, 1)][0]
        own_rows = matmul(chosen_rows, held).astype(BF16)
        averaged = (matmul(tally_rows, held) * share_rows).astype(BF16)
        weight = proj[pl.ds(index, 1)][0]
        preact_ref[...] += matmul(own_rows, weight[0]) + matmul(averaged, weight[1])

    preact = preact_ref[...]
    square = preact * preact
    bent = jnp.tanh(0.7978845608 * (preact + 0.044715 * preact * square))
    rise = 0.7978845608 * (1.0 + 3.0 * 0.044715 * square)
    half = 0.5 * (1.0 + bent)
    loads[7].wait()
    slope = upstream[...].astype(F32) * (half + 0.5 * preact * (1.0 - bent * bent) * rise)
    both = matmul(back, slope.astype(BF16))
    own_terms[0] = both[:slots].astype(BF16)
    own_terms[1] = (both[slots : 2 * slots] + both[2 * slots :]).astype(BF16)
    keep = pltpu.make_async_copy(own_terms, terms.at[mine, me], local_sem.at[8])
    keep.start()

    flip_y, flip_x, flip_core = 1 - y, 1 - x, 1 - core
    depths = [z] + [lax.rem(z + k, depth) for k in range(1, depth)]
    counter = [0]

    def pass_on(node, feat, to_node, to_feat, src=None):
        copy = remote(
            terms.at[feat, node] if src is None else src,
            terms.at[feat, node],
            term_send.at[counter[0]],
            term_recv.at[feat, node],
            to_node,
            to_feat,
        )
        counter[0] += 1
        copy.start()
        sends.append(copy)

    def arrived(node, feat):
        remote(
            terms.at[feat, node],
            terms.at[feat, node],
            term_send.at[0],
            term_recv.at[feat, node],
            me,
            2 * x + flip_core,
        ).wait_recv()

    to_y = (2 * z + flip_y, mine)
    to_x = (me, 2 * flip_x + core)
    to_core = (me, 2 * x + flip_core)
    for k in range(1, depth):
        pass_on(me, mine, 2 * depths[k] + y, mine, own_terms)
    for k in range(depth):
        node = 2 * depths[k] + y
        if k > 0:
            arrived(node, mine)
        for target in (to_y, to_x, to_core):
            pass_on(node, mine, *target, src=own_terms if k == 0 else None)

    hid_out[...] = (preact * half).astype(BF16)

    def out_rows(index):
        return hid_out.at[pl.ds(pl.multiple_of(index * portion, portion), portion), :]

    for k, peer in enumerate(feat_peers):
        copy = remote(out_rows(peer), hidden_ref.at[mine], hid_send.at[k], hid_recv.at[mine], me, peer)
        copy.start()
        sends.append(copy)
    keep_rows = pltpu.make_async_copy(out_rows(mine), hidden_ref.at[mine], local_sem.at[9])
    keep_rows.start()

    across = 2 * flip_x + core
    early = depth // 2
    for k in range(depth):
        node_y, node_x = 2 * depths[k] + flip_y, 2 * depths[k] + y
        arrived(node_y, mine)
        if k < early:
            pass_on(node_y, mine, *to_x)
        arrived(node_x, across)
        if k >= early:
            pass_on(node_x, across, *to_y)
        pass_on(node_y, mine, *to_core)
        pass_on(node_x, across, *to_core)

    for k in range(depth):
        node = 2 * depths[k] + flip_y
        arrived(node, across)
        pass_on(node, across, *to_core)
    for feat in (2 * x + flip_core, 2 * flip_x + flip_core):
        for node in range(nodes):
            arrived(node, feat)
    for peer in feat_peers:
        remote(hidden_ref.at[peer], hidden_ref.at[peer], hid_send.at[0], hid_recv.at[peer], me, peer).wait_recv()
    for copy in sends:
        copy.wait_send()
    keep.wait()
    keep_rows.wait()


def gradient_kernel(hidden_in, terms, ordered, hidden_ref, grad_ref, rows_out, grad, out_sem):
    feats, nodes, layers, slots, width = terms.shape
    for k in range(feats):
        rows_out[:, k * width : (k + 1) * width] = hidden_in[k]
    keep_rows = pltpu.make_async_copy(rows_out, hidden_ref, out_sem.at[feats])
    keep_rows.start()

    def part(feat):
        columns = pl.ds(pl.multiple_of(feat * width, width), width)
        return pltpu.make_async_copy(grad.at[feat], grad_ref.at[:, :, columns], out_sem.at[feat])

    @pl.loop(0, feats)
    def _(feat):
        held = terms[pl.ds(feat, 1)][0]
        for layer in range(layers):
            total = matmul(ordered[...], held[:, layer].reshape(nodes * slots, width))
            grad[pl.ds(feat, 1), layer : layer + 1] = total[None, None]
        part(feat).start()

    @pl.loop(0, feats)
    def _(feat):
        part(feat).wait()

    keep_rows.wait()


def compact_step(
    feature_table,
    weights,
    request_rows,
    request_counts,
    neighbors,
    nbr_counts,
    self_rows,
    grad_hidden,
):
    nodes, feats = lax.axis_size("node"), lax.axis_size("feat")
    caps, fan = request_rows.shape[2], neighbors.shape[1]
    slots = nodes * caps
    targets, hidden = grad_hidden.shape
    rows, features = feature_table.shape
    width, portion = hidden // feats, targets // feats
    dma = pltpu.SemaphoreType.DMA
    vmem = pl.BlockSpec(memory_space=pltpu.VMEM)
    anywhere = pl.BlockSpec(memory_space=pl.ANY)
    moves = nodes * feats - 1
    hidden_in, terms, ordered = pl.pallas_call(
        functools.partial(step_kernel, (nodes, feats, caps, fan)),
        out_shape=(
            jax.ShapeDtypeStruct((feats, portion, width), BF16),
            jax.ShapeDtypeStruct((feats, nodes, 2, slots, width), BF16),
            jax.ShapeDtypeStruct((features, nodes * slots), BF16),
        ),
        in_specs=[pl.BlockSpec(memory_space=pltpu.HBM)] * 8,
        out_specs=(anywhere, anywhere, vmem),
        scratch_shapes=[
            pltpu.VMEM((caps, 1, nodes), jnp.int32),
            pltpu.VMEM((1, nodes), jnp.int32),
            pltpu.VMEM((fan, targets), jnp.int32),
            pltpu.VMEM((1, targets), jnp.int32),
            pltpu.VMEM((1, targets), jnp.int32),
            pltpu.VMEM((features, rows), BF16),
            pltpu.VMEM((targets, width), BF16),
            pltpu.VMEM((8, 128), jnp.int32),
            pltpu.VMEM((nodes, 8, 128), jnp.int32),
            pltpu.VMEM((slots, 128), jnp.int32),
            pltpu.VMEM((nodes, slots, features), BF16),
            pltpu.VMEM((feats, slots, features), BF16),
            pltpu.VMEM((feats, 2, features, width), BF16),
            pltpu.VMEM((targets, width), F32),
            pltpu.VMEM((targets, width), BF16),
            pltpu.VMEM((2, slots, width), BF16),
            pltpu.VMEM((nodes * slots, features), BF16),
            dma((10,)),
            dma((nodes,)),
            dma((nodes,)),
            dma((nodes,)),
            dma((nodes,)),
            dma((feats,)),
            dma((feats,)),
            dma((feats,)),
            dma((feats,)),
            dma((feats,)),
            dma((feats,)),
            dma((moves,)),
            dma((feats, nodes)),
        ],
        compiler_params=pltpu.CompilerParams(
            collective_id=0, has_side_effects=True, vmem_limit_bytes=24 * 1024 * 1024
        ),
    )(
        *(
            pltpu.with_memory_space_constraint(operand, pltpu.HBM)
            for operand in (
                request_rows.transpose(2, 0, 1),
                request_counts,
                neighbors.T,
                nbr_counts[None],
                self_rows[None],
                feature_table.T,
                weights,
                grad_hidden,
            )
        )
    )
    hbm = pl.BlockSpec(memory_space=pltpu.HBM)
    return pl.pallas_call(
        gradient_kernel,
        out_shape=(
            jax.ShapeDtypeStruct((portion, hidden), BF16),
            jax.ShapeDtypeStruct((2, features, hidden), F32),
        ),
        in_specs=[vmem, vmem, vmem],
        out_specs=(hbm, hbm),
        scratch_shapes=[
            pltpu.VMEM((portion, hidden), BF16),
            pltpu.VMEM((feats, 2, features, width), F32),
            dma((feats + 1,)),
        ],
        compiler_params=pltpu.CompilerParams(vmem_limit_bytes=24 * 1024 * 1024),
    )(hidden_in, terms, ordered)


def smooth_gate(values):
    return (
        0.5
        * values
        * (1.0 + jnp.tanh(0.7978845608 * (values + 0.044715 * values * values * values)))
    )


def activate(preact, upstream):
    output, pullback = jax.vjp(smooth_gate, preact)
    slope = pullback(upstream.astype(jnp.float32))[0]
    return (output.astype(jnp.bfloat16), slope.astype(jnp.bfloat16))


def aggregate(frontier, local_nbrs, local_counts):
    picked = frontier[local_nbrs]
    within = jnp.arange(local_nbrs.shape[1], dtype=jnp.int32)[None, :] < local_counts[:, None]
    summed = jnp.sum(
        jnp.where(within[:, :, None], picked, jnp.zeros_like(picked)), axis=1, dtype=jnp.float32
    )
    return (summed / local_counts[:, None].astype(jnp.float32)).astype(jnp.bfloat16)


def project(own_rows, averaged, weights):
    first = jnp.dot(own_rows, weights[0], preferred_element_type=jnp.float32)
    return first + jnp.dot(averaged, weights[1], preferred_element_type=jnp.float32)


def contract(left_side, right_side):
    return lax.dot_general(
        left_side, right_side, (((0,), (0,)), ((), ())), preferred_element_type=jnp.float32
    )


def per_device(
    feature_table,
    weights,
    request_rows,
    request_counts,
    neighbors,
    nbr_counts,
    self_rows,
    grad_hidden,
):
    slot_count = request_rows.shape[2]
    looked = feature_table[
        lax.all_to_all(request_rows[0], "node", split_axis=0, concat_axis=0, tiled=True)
    ]
    fetched = lax.all_to_all(looked, "node", split_axis=0, concat_axis=0, tiled=True)
    filled = jnp.arange(slot_count, dtype=jnp.int32)[None, :] < request_counts[0][:, None]
    frontier = jnp.where(filled[:, :, None], fetched, jnp.zeros_like(fetched)).reshape(
        -1, fetched.shape[2]
    )
    own_rows = frontier[self_rows]
    averaged = aggregate(frontier, neighbors, nbr_counts)
    groups = lax.axis_size("feat")
    portion = own_rows.shape[0] // groups
    preact = lax.psum(project(own_rows, averaged, weights), "feat")
    output_all, slope = activate(preact, grad_hidden)
    hidden = lax.dynamic_slice_in_dim(output_all, lax.axis_index("feat") * portion, portion, 0)
    grad_terms = jnp.stack([contract(own_rows, slope), contract(averaged, slope)])
    weight_grad = lax.psum(grad_terms, "node")
    return (hidden, weight_grad)


def solution(mesh):
    placed = (
        P("node", "feat"),
        P(None, "feat", None),
        P("node", None, None),
        P("node", None),
        P("node", None),
        P("node"),
        P("node"),
        P("node", None),
    )
    nodes, feats = mesh.shape["node"], mesh.shape["feat"]

    def per_slice(feature_table, weights, request_rows, *others):
        slots = nodes * request_rows.shape[2]
        plan = per_device
        if feats == 4 and nodes % 2 == 0 and slots % 16 == 0 and slots <= 128 and request_rows.shape[2] <= 8:
            plan = compact_step
        return plan(feature_table, weights, request_rows, *others)

    return jax.shard_map(
        per_slice,
        mesh=mesh,
        in_specs=placed,
        out_specs=(P(("node", "feat"), None), P(None, "feat", None)),
        check_vma=False,
    )
```

```python
import functools

import jax
import jax.numpy as jnp
from jax import lax
from jax.experimental import pallas as pl
from jax.experimental.pallas import tpu as pltpu
from jax.sharding import PartitionSpec as P

MESH = pl.DeviceIdType.MESH
F32, BF16 = jnp.float32, jnp.bfloat16


def matmul(left, right):
    return jnp.dot(left, right, preferred_element_type=F32)


def step_kernel(
    sizes,
    request_ref,
    counts_ref,
    nbrs_ref,
    nbr_counts_ref,
    self_ref,
    table_ref,
    weights_ref,
    upstream_ref,
    hidden_ref,
    terms,
    ordered_ref,
    request,
    counts,
    nbrs,
    nbr_counts,
    self_rows,
    table,
    upstream,
    ask_out,
    asked,
    look_out,
    look_in,
    front,
    proj,
    preact_ref,
    hid_out,
    own_terms,
    in_order,
    local_sem,
    ask_send,
    ask_recv,
    look_send,
    look_recv,
    front_send,
    front_recv,
    order_send,
    order_recv,
    proj_send,
    proj_recv,
    hid_send,
    hid_recv,
    term_send,
    term_recv,
):
    nodes, feats, caps, fan = sizes
    slots = nodes * caps
    depth = nodes // 2
    portion = hidden_ref.shape[1]
    width = hidden_ref.shape[2]
    me, mine = lax.axis_index("node"), lax.axis_index("feat")
    z, y, x, core = me // 2, me % 2, mine // 2, mine % 2
    node_peers = [lax.rem(me + k, nodes) for k in range(1, nodes)]
    feat_peers = [lax.rem(mine + k, feats) for k in range(1, feats)]
    my_columns = pl.ds(pl.multiple_of(mine * width, width), width)

    def columns(index):
        return pl.ds(pl.multiple_of(index * width, width), width)

    def remote(src, dst, send, recv, node, feat):
        return pltpu.make_async_remote_copy(
            src_ref=src,
            dst_ref=dst,
            send_sem=send,
            recv_sem=recv,
            device_id=(node, feat),
            device_id_type=MESH,
        )

    loads = []
    for k, (src, dst) in enumerate(
        (
            (request_ref, request),
            (nbrs_ref, nbrs),
            (nbr_counts_ref, nbr_counts),
            (self_ref, self_rows),
            (counts_ref, counts),
            (table_ref, table),
            (weights_ref.at[:, :, my_columns], proj.at[mine]),
            (upstream_ref.at[:, my_columns], upstream),
        )
    ):
        copy = pltpu.make_async_copy(src, dst, local_sem.at[k])
        copy.start()
        loads.append(copy)

    barrier = pltpu.get_barrier_semaphore()
    for peer in node_peers:
        pl.semaphore_signal(barrier, inc=1, device_id=(peer, mine), device_id_type=MESH)
    for peer in feat_peers:
        pl.semaphore_signal(barrier, inc=1, device_id=(me, peer), device_id_type=MESH)

    ask_out[...] = jnp.zeros_like(ask_out)
    loads[0].wait()
    for k in range(caps):
        ask_out[k : k + 1, 0:nodes] = request[k]
    pl.semaphore_wait(barrier, nodes + feats - 2)

    sends = []
    for k, peer in enumerate(node_peers):
        copy = remote(ask_out, asked.at[me], ask_send.at[k], ask_recv.at[me], peer, mine)
        copy.start()
        sends.append(copy)
    flip_y, flip_x, flip_core = 1 - y, 1 - x, 1 - core
    sibling = 2 * x + flip_core
    across = (2 * flip_x + core, 2 * flip_x + flip_core)
    for k, peer in enumerate(across):
        copy = remote(
            weights_ref.at[y, :, columns(peer)],
            proj.at[mine, y],
            proj_send.at[k],
            proj_recv.at[mine, y],
            me,
            peer,
        )
        copy.start()
        sends.append(copy)
    copy = remote(
        weights_ref.at[:, :, columns(sibling)],
        proj.at[mine],
        proj_send.at[2],
        proj_recv.at[mine, 0],
        me,
        sibling,
    )
    copy.start()
    sends.append(copy)
    asked[pl.ds(me, 1)] = ask_out[...][None]

    for copy in loads[1:5]:
        copy.wait()
    targets = nbrs.shape[1]

    def owner_of(slot):
        owner = jnp.zeros_like(slot)
        for k in range(1, nodes):
            owner = owner + (slot >= k * caps).astype(jnp.int32)
        return owner

    held_by = owner_of(lax.broadcasted_iota(jnp.int32, (slots, nodes), 0))
    here = lax.broadcasted_iota(jnp.int32, (slots, nodes), 1) == held_by
    limit = jnp.sum(
        jnp.where(here, counts[...].astype(F32), 0.0), axis=1, keepdims=True
    )
    slot = lax.broadcasted_iota(jnp.int32, (slots, targets), 0)
    live = (slot - owner_of(slot) * caps).astype(F32) < limit
    chosen = jnp.where(live & (slot == self_rows[...]), 1.0, 0.0).astype(F32)
    valid = nbr_counts[...]
    tally = jnp.zeros((slots, targets), F32)
    for k in range(fan):
        tally = tally + jnp.where((slot == nbrs[k : k + 1, :]) & (valid > k), 1.0, 0.0)
    tally = jnp.where(live, tally, 0.0)
    share = 1.0 / valid.astype(F32)
    mean = tally * share
    mean_high = mean.astype(BF16)
    mean_low = (mean - mean_high.astype(F32)).astype(BF16)
    back = jnp.concatenate([chosen.astype(BF16), mean_high, mean_low], axis=0)
    chosen_rows = chosen.T.astype(BF16)
    tally_rows = tally.T.astype(BF16)
    share_rows = jnp.broadcast_to(share, (128, targets)).T[:, 0:1]

    for peer in node_peers:
        remote(asked.at[peer], asked.at[peer], ask_send.at[0], ask_recv.at[peer], peer, mine).wait_recv()
    numbers = asked[...].reshape(nodes * 8, 128).astype(F32)
    lane = lax.broadcasted_iota(jnp.int32, numbers.shape, 1)
    wanted = jnp.sum(jnp.where(lane == me, numbers, 0.0), axis=1, keepdims=True)
    wanted = wanted.astype(jnp.int32)
    rows = table.shape[1]
    pick = (lax.broadcasted_iota(jnp.int32, (nodes * 8, rows), 1) == wanted).astype(F32)
    loads[5].wait()
    found = lax.dot_general(
        pick.astype(BF16), table[...], (((1,), (1,)), ((), ())), preferred_element_type=F32
    )
    look_out[...] = found.reshape(look_out.shape)
    for k, peer in enumerate(node_peers):
        copy = remote(look_out.at[peer], look_in.at[me], look_send.at[k], look_recv.at[me], peer, mine)
        copy.start()
        sends.append(copy)
    look_in[pl.ds(me, 1)] = look_out[pl.ds(me, 1)]

    def piece(index, layer):
        return remote(
            proj.at[index, layer],
            proj.at[index, layer],
            proj_send.at[0],
            proj_recv.at[index, layer],
            2 * z + flip_y,
            mine,
        )

    for k, peer in enumerate(across):
        piece(peer, y).wait_recv()
        copy = remote(
            proj.at[peer, y],
            proj.at[peer, y],
            proj_send.at[3 + k],
            proj_recv.at[peer, y],
            2 * z + flip_y,
            mine,
        )
        copy.start()
        sends.append(copy)
    for peer in node_peers:
        remote(look_in.at[peer], look_in.at[peer], look_send.at[0], look_recv.at[peer], peer, mine).wait_recv()

    row = lax.broadcasted_iota(jnp.int32, (slots, nodes * 8), 0)
    col = lax.broadcasted_iota(jnp.int32, (slots, nodes * 8), 1)
    block = owner_of(row)
    pack = (col == block * 8 + (row - block * caps)).astype(F32).astype(BF16)
    own_front = matmul(pack, look_in[...].reshape(nodes * 8, look_in.shape[2]).astype(BF16))
    front[pl.ds(mine, 1)] = own_front.astype(BF16)[None]
    in_order[pl.ds(me, 1)] = own_front.astype(BF16)[None]
    for k, peer in enumerate(feat_peers):
        copy = remote(front.at[mine], front.at[mine], front_send.at[k], front_recv.at[mine], me, peer)
        copy.start()
        sends.append(copy)

    for k, peer in enumerate(node_peers):
        copy = remote(
            front.at[mine], in_order.at[me], order_send.at[k], order_recv.at[me], peer, mine
        )
        copy.start()
        sends.append(copy)

    loads[6].wait()
    preact_ref[...] = jnp.zeros_like(preact_ref)

    @pl.loop(0, feats)
    def _(k):
        index = 2 * lax.rem(x + k // 2, 2) + lax.rem(core + lax.rem(k, 2), 2)

        @pl.when(k > 0)
        def _():
            remote(front.at[index], front.at[index], front_send.at[0], front_recv.at[index], me, index).wait_recv()

        @pl.when(k == 1)
        def _():
            remote(proj.at[index], proj.at[index], proj_send.at[0], proj_recv.at[index, 0], me, index).wait_recv()

        @pl.when(k > 1)
        def _():
            piece(index, flip_y).wait_recv()

        held = front[pl.ds(index, 1)][0]
        own_rows = matmul(chosen_rows, held).astype(BF16)
        averaged = (matmul(tally_rows, held) * share_rows).astype(BF16)
        weight = proj[pl.ds(index, 1)][0]
        preact_ref[...] += matmul(own_rows, weight[0]) + matmul(averaged, weight[1])

    preact = preact_ref[...]
    square = preact * preact
    bent = jnp.tanh(0.7978845608 * (preact + 0.044715 * preact * square))
    rise = 0.7978845608 * (1.0 + 3.0 * 0.044715 * square)
    half = 0.5 * (1.0 + bent)
    loads[7].wait()
    slope = upstream[...].astype(F32) * (half + 0.5 * preact * (1.0 - bent * bent) * rise)
    both = matmul(back, slope.astype(BF16))
    own_terms[0] = both[:slots].astype(BF16)
    own_terms[1] = (both[slots : 2 * slots] + both[2 * slots :]).astype(BF16)
    keep = pltpu.make_async_copy(own_terms, terms.at[mine, me], local_sem.at[8])
    keep.start()

    depths = [z] + [lax.rem(z + k, depth) for k in range(1, depth)]
    counter = [0]

    def pass_on(node, feat, to_node, to_feat, src=None):
        copy = remote(
            terms.at[feat, node] if src is None else src,
            terms.at[feat, node],
            term_send.at[counter[0]],
            term_recv.at[feat, node],
            to_node,
            to_feat,
        )
        counter[0] += 1
        copy.start()
        sends.append(copy)

    def arrived(node, feat):
        remote(
            terms.at[feat, node],
            terms.at[feat, node],
            term_send.at[0],
            term_recv.at[feat, node],
            me,
            2 * x + flip_core,
        ).wait_recv()

    to_y = (2 * z + flip_y, mine)
    to_x = (me, 2 * flip_x + core)
    to_core = (me, 2 * x + flip_core)
    for k in range(1, depth):
        pass_on(me, mine, 2 * depths[k] + y, mine, own_terms)
    for k in range(depth):
        node = 2 * depths[k] + y
        if k > 0:
            arrived(node, mine)
        for target in (to_y, to_x, to_core):
            pass_on(node, mine, *target, src=own_terms if k == 0 else None)

    hid_out[...] = (preact * half).astype(BF16)

    def out_rows(index):
        return hid_out.at[pl.ds(pl.multiple_of(index * portion, portion), portion), :]

    for k, peer in enumerate(feat_peers):
        copy = remote(out_rows(peer), hidden_ref.at[mine], hid_send.at[k], hid_recv.at[mine], me, peer)
        copy.start()
        sends.append(copy)
    keep_rows = pltpu.make_async_copy(out_rows(mine), hidden_ref.at[mine], local_sem.at[9])
    keep_rows.start()

    for peer in node_peers:
        remote(in_order.at[peer], in_order.at[peer], order_send.at[0], order_recv.at[peer], peer, mine).wait_recv()
    ordered_ref[...] = in_order[...].reshape(nodes * slots, in_order.shape[2]).T

    across = across[0]
    early = depth // 2
    for k in range(depth):
        node_y, node_x = 2 * depths[k] + flip_y, 2 * depths[k] + y
        arrived(node_y, mine)
        if k < early:
            pass_on(node_y, mine, *to_x)
        arrived(node_x, across)
        if k >= early:
            pass_on(node_x, across, *to_y)
        pass_on(node_y, mine, *to_core)
        pass_on(node_x, across, *to_core)

    for k in range(depth):
        node = 2 * depths[k] + flip_y
        arrived(node, across)
        pass_on(node, across, *to_core)
    for feat in (2 * x + flip_core, 2 * flip_x + flip_core):
        for node in range(nodes):
            arrived(node, feat)
    for peer in feat_peers:
        remote(hidden_ref.at[peer], hidden_ref.at[peer], hid_send.at[0], hid_recv.at[peer], me, peer).wait_recv()
    for copy in sends:
        copy.wait_send()
    keep.wait()
    keep_rows.wait()


def gradient_kernel(hidden_in, terms, ordered, hidden_ref, grad_ref, rows_out, grad, out_sem):
    feats, nodes, layers, slots, width = terms.shape
    for k in range(feats):
        rows_out[:, k * width : (k + 1) * width] = hidden_in[k]
    keep_rows = pltpu.make_async_copy(rows_out, hidden_ref, out_sem.at[feats])
    keep_rows.start()

    def part(feat):
        columns = pl.ds(pl.multiple_of(feat * width, width), width)
        return pltpu.make_async_copy(grad.at[feat], grad_ref.at[:, :, columns], out_sem.at[feat])

    @pl.loop(0, feats)
    def _(feat):
        held = terms[pl.ds(feat, 1)][0]
        for layer in range(layers):
            total = matmul(ordered[...], held[:, layer].reshape(nodes * slots, width))
            grad[pl.ds(feat, 1), layer : layer + 1] = total[None, None]
        part(feat).start()

    @pl.loop(0, feats)
    def _(feat):
        part(feat).wait()

    keep_rows.wait()


def compact_step(
    feature_table,
    weights,
    request_rows,
    request_counts,
    neighbors,
    nbr_counts,
    self_rows,
    grad_hidden,
):
    nodes, feats = lax.axis_size("node"), lax.axis_size("feat")
    caps, fan = request_rows.shape[2], neighbors.shape[1]
    slots = nodes * caps
    targets, hidden = grad_hidden.shape
    rows, features = feature_table.shape
    width, portion = hidden // feats, targets // feats
    dma = pltpu.SemaphoreType.DMA
    vmem = pl.BlockSpec(memory_space=pltpu.VMEM)
    anywhere = pl.BlockSpec(memory_space=pl.ANY)
    moves = nodes * feats - 1
    hidden_in, terms, ordered = pl.pallas_call(
        functools.partial(step_kernel, (nodes, feats, caps, fan)),
        out_shape=(
            jax.ShapeDtypeStruct((feats, portion, width), BF16),
            jax.ShapeDtypeStruct((feats, nodes, 2, slots, width), BF16),
            jax.ShapeDtypeStruct((features, nodes * slots), BF16),
        ),
        in_specs=[pl.BlockSpec(memory_space=pltpu.HBM)] * 8,
        out_specs=(anywhere, anywhere, vmem),
        scratch_shapes=[
            pltpu.VMEM((caps, 1, nodes), jnp.int32),
            pltpu.VMEM((1, nodes), jnp.int32),
            pltpu.VMEM((fan, targets), jnp.int32),
            pltpu.VMEM((1, targets), jnp.int32),
            pltpu.VMEM((1, targets), jnp.int32),
            pltpu.VMEM((features, rows), BF16),
            pltpu.VMEM((targets, width), BF16),
            pltpu.VMEM((8, 128), jnp.int32),
            pltpu.VMEM((nodes, 8, 128), jnp.int32),
            pltpu.VMEM((nodes, 8, features), F32),
            pltpu.VMEM((nodes, 8, features), F32),
            pltpu.VMEM((feats, slots, features), BF16),
            pltpu.VMEM((feats, 2, features, width), BF16),
            pltpu.VMEM((targets, width), F32),
            pltpu.VMEM((targets, width), BF16),
            pltpu.VMEM((2, slots, width), BF16),
            pltpu.VMEM((nodes, slots, features), BF16),
            dma((10,)),
            dma((nodes,)),
            dma((nodes,)),
            dma((nodes,)),
            dma((nodes,)),
            dma((feats,)),
            dma((feats,)),
            dma((nodes,)),
            dma((nodes,)),
            dma((5,)),
            dma((feats, 2)),
            dma((feats,)),
            dma((feats,)),
            dma((moves,)),
            dma((feats, nodes)),
        ],
        compiler_params=pltpu.CompilerParams(
            collective_id=0, has_side_effects=True, vmem_limit_bytes=24 * 1024 * 1024
        ),
    )(
        *(
            pltpu.with_memory_space_constraint(operand, pltpu.HBM)
            for operand in (
                request_rows.transpose(2, 0, 1),
                request_counts,
                neighbors.T,
                nbr_counts[None],
                self_rows[None],
                feature_table.T,
                weights,
                grad_hidden,
            )
        )
    )
    hbm = pl.BlockSpec(memory_space=pltpu.HBM)
    return pl.pallas_call(
        gradient_kernel,
        out_shape=(
            jax.ShapeDtypeStruct((portion, hidden), BF16),
            jax.ShapeDtypeStruct((2, features, hidden), F32),
        ),
        in_specs=[vmem, vmem, vmem],
        out_specs=(hbm, hbm),
        scratch_shapes=[
            pltpu.VMEM((portion, hidden), BF16),
            pltpu.VMEM((feats, 2, features, width), F32),
            dma((feats + 1,)),
        ],
        compiler_params=pltpu.CompilerParams(vmem_limit_bytes=24 * 1024 * 1024),
    )(hidden_in, terms, ordered)


def smooth_gate(values):
    return (
        0.5
        * values
        * (1.0 + jnp.tanh(0.7978845608 * (values + 0.044715 * values * values * values)))
    )


def activate(preact, upstream):
    output, pullback = jax.vjp(smooth_gate, preact)
    slope = pullback(upstream.astype(jnp.float32))[0]
    return (output.astype(jnp.bfloat16), slope.astype(jnp.bfloat16))


def aggregate(frontier, local_nbrs, local_counts):
    picked = frontier[local_nbrs]
    within = jnp.arange(local_nbrs.shape[1], dtype=jnp.int32)[None, :] < local_counts[:, None]
    summed = jnp.sum(
        jnp.where(within[:, :, None], picked, jnp.zeros_like(picked)), axis=1, dtype=jnp.float32
    )
    return (summed / local_counts[:, None].astype(jnp.float32)).astype(jnp.bfloat16)


def project(own_rows, averaged, weights):
    first = jnp.dot(own_rows, weights[0], preferred_element_type=jnp.float32)
    return first + jnp.dot(averaged, weights[1], preferred_element_type=jnp.float32)


def contract(left_side, right_side):
    return lax.dot_general(
        left_side, right_side, (((0,), (0,)), ((), ())), preferred_element_type=jnp.float32
    )


def per_device(
    feature_table,
    weights,
    request_rows,
    request_counts,
    neighbors,
    nbr_counts,
    self_rows,
    grad_hidden,
):
    slot_count = request_rows.shape[2]
    looked = feature_table[
        lax.all_to_all(request_rows[0], "node", split_axis=0, concat_axis=0, tiled=True)
    ]
    fetched = lax.all_to_all(looked, "node", split_axis=0, concat_axis=0, tiled=True)
    filled = jnp.arange(slot_count, dtype=jnp.int32)[None, :] < request_counts[0][:, None]
    frontier = jnp.where(filled[:, :, None], fetched, jnp.zeros_like(fetched)).reshape(
        -1, fetched.shape[2]
    )
    own_rows = frontier[self_rows]
    averaged = aggregate(frontier, neighbors, nbr_counts)
    groups = lax.axis_size("feat")
    portion = own_rows.shape[0] // groups
    preact = lax.psum(project(own_rows, averaged, weights), "feat")
    output_all, slope = activate(preact, grad_hidden)
    hidden = lax.dynamic_slice_in_dim(output_all, lax.axis_index("feat") * portion, portion, 0)
    grad_terms = jnp.stack([contract(own_rows, slope), contract(averaged, slope)])
    weight_grad = lax.psum(grad_terms, "node")
    return (hidden, weight_grad)


def solution(mesh):
    placed = (
        P("node", "feat"),
        P(None, "feat", None),
        P("node", None, None),
        P("node", None),
        P("node", None),
        P("node"),
        P("node"),
        P("node", None),
    )
    nodes, feats = mesh.shape["node"], mesh.shape["feat"]

    def per_slice(feature_table, weights, request_rows, *others):
        slots = nodes * request_rows.shape[2]
        plan = per_device
        if feats == 4 and nodes % 2 == 0 and slots % 16 == 0 and slots <= 128 and request_rows.shape[2] <= 8:
            plan = compact_step
        return plan(feature_table, weights, request_rows, *others)

    return jax.shard_map(
        per_slice,
        mesh=mesh,
        in_specs=placed,
        out_specs=(P(("node", "feat"), None), P(None, "feat", None)),
        check_vma=False,
    )
```

```python
import functools

import jax
import jax.numpy as jnp
from jax import lax
from jax.experimental import pallas as pl
from jax.experimental.pallas import tpu as pltpu
from jax.sharding import PartitionSpec as P

MESH = pl.DeviceIdType.MESH
F32, BF16 = jnp.float32, jnp.bfloat16


def matmul(left, right):
    return jnp.dot(left, right, preferred_element_type=F32)


def step_kernel(
    sizes,
    request_ref,
    counts_ref,
    nbrs_ref,
    nbr_counts_ref,
    self_ref,
    table_ref,
    weights_ref,
    upstream_ref,
    hidden_ref,
    terms,
    ordered_ref,
    request,
    counts,
    nbrs,
    nbr_counts,
    self_rows,
    table,
    upstream,
    ask_out,
    asked,
    look_out,
    look_in,
    front,
    proj,
    preact_ref,
    hid_out,
    own_terms,
    in_order,
    local_sem,
    ask_send,
    ask_recv,
    look_send,
    look_recv,
    front_send,
    front_recv,
    order_send,
    order_recv,
    proj_send,
    proj_recv,
    hid_send,
    hid_recv,
    term_send,
    term_recv,
):
    nodes, feats, caps, fan = sizes
    slots = nodes * caps
    depth = nodes // 2
    portion = hidden_ref.shape[1]
    width = hidden_ref.shape[2]
    me, mine = lax.axis_index("node"), lax.axis_index("feat")
    z, y, x, core = me // 2, me % 2, mine // 2, mine % 2
    node_peers = [lax.rem(me + k, nodes) for k in range(1, nodes)]
    feat_peers = [lax.rem(mine + k, feats) for k in range(1, feats)]
    my_columns = pl.ds(pl.multiple_of(mine * width, width), width)

    def columns(index):
        return pl.ds(pl.multiple_of(index * width, width), width)

    def remote(src, dst, send, recv, node, feat):
        return pltpu.make_async_remote_copy(
            src_ref=src,
            dst_ref=dst,
            send_sem=send,
            recv_sem=recv,
            device_id=(node, feat),
            device_id_type=MESH,
        )

    loads = []
    for k, (src, dst) in enumerate(
        (
            (request_ref, request),
            (nbrs_ref, nbrs),
            (nbr_counts_ref, nbr_counts),
            (self_ref, self_rows),
            (counts_ref, counts),
            (table_ref, table),
            (weights_ref.at[:, :, my_columns], proj.at[mine]),
            (upstream_ref.at[:, my_columns], upstream),
        )
    ):
        copy = pltpu.make_async_copy(src, dst, local_sem.at[k])
        copy.start()
        loads.append(copy)

    barrier = pltpu.get_barrier_semaphore()
    for peer in node_peers:
        pl.semaphore_signal(barrier, inc=1, device_id=(peer, mine), device_id_type=MESH)
    for peer in feat_peers:
        pl.semaphore_signal(barrier, inc=1, device_id=(me, peer), device_id_type=MESH)

    ask_out[...] = jnp.zeros_like(ask_out)
    loads[0].wait()
    for k in range(caps):
        ask_out[k : k + 1, 0:nodes] = request[k]
    pl.semaphore_wait(barrier, nodes + feats - 2)

    sends = []
    for k, peer in enumerate(node_peers):
        copy = remote(ask_out, asked.at[me], ask_send.at[k], ask_recv.at[me], peer, mine)
        copy.start()
        sends.append(copy)
    flip_y, flip_x, flip_core = 1 - y, 1 - x, 1 - core
    sibling = 2 * x + flip_core
    across = (2 * flip_x + core, 2 * flip_x + flip_core)
    for k, peer in enumerate(across):
        copy = remote(
            weights_ref.at[y, :, columns(peer)],
            proj.at[mine, y],
            proj_send.at[k],
            proj_recv.at[mine, y],
            me,
            peer,
        )
        copy.start()
        sends.append(copy)
    copy = remote(
        weights_ref.at[:, :, columns(sibling)],
        proj.at[mine],
        proj_send.at[2],
        proj_recv.at[mine, 0],
        me,
        sibling,
    )
    copy.start()
    sends.append(copy)
    asked[pl.ds(me, 1)] = ask_out[...][None]

    for copy in loads[1:5]:
        copy.wait()
    targets = nbrs.shape[1]

    def owner_of(slot):
        owner = jnp.zeros_like(slot)
        for k in range(1, nodes):
            owner = owner + (slot >= k * caps).astype(jnp.int32)
        return owner

    held_by = owner_of(lax.broadcasted_iota(jnp.int32, (slots, nodes), 0))
    here = lax.broadcasted_iota(jnp.int32, (slots, nodes), 1) == held_by
    limit = jnp.sum(
        jnp.where(here, counts[...].astype(F32), 0.0), axis=1, keepdims=True
    )
    slot = lax.broadcasted_iota(jnp.int32, (slots, targets), 0)
    live = (slot - owner_of(slot) * caps).astype(F32) < limit
    chosen = jnp.where(live & (slot == self_rows[...]), 1.0, 0.0).astype(F32)
    valid = nbr_counts[...]
    tally = jnp.zeros((slots, targets), F32)
    for k in range(fan):
        tally = tally + jnp.where((slot == nbrs[k : k + 1, :]) & (valid > k), 1.0, 0.0)
    tally = jnp.where(live, tally, 0.0)
    share = 1.0 / valid.astype(F32)
    mean = tally * share
    mean_high = mean.astype(BF16)
    mean_low = (mean - mean_high.astype(F32)).astype(BF16)
    back = jnp.concatenate([chosen.astype(BF16), mean_high, mean_low], axis=0)
    chosen_rows = chosen.T.astype(BF16)
    tally_rows = tally.T.astype(BF16)
    share_rows = jnp.broadcast_to(share, (128, targets)).T[:, 0:1]

    for peer in node_peers:
        remote(asked.at[peer], asked.at[peer], ask_send.at[0], ask_recv.at[peer], peer, mine).wait_recv()
    numbers = asked[...].reshape(nodes * 8, 128).astype(F32)
    lane = lax.broadcasted_iota(jnp.int32, numbers.shape, 1)
    wanted = jnp.sum(jnp.where(lane == me, numbers, 0.0), axis=1, keepdims=True)
    wanted = wanted.astype(jnp.int32)
    rows = table.shape[1]
    pick = (lax.broadcasted_iota(jnp.int32, (nodes * 8, rows), 1) == wanted).astype(F32)
    loads[5].wait()
    found = lax.dot_general(
        pick.astype(BF16), table[...], (((1,), (1,)), ((), ())), preferred_element_type=F32
    )
    look_out[...] = found.reshape(look_out.shape)
    for k, peer in enumerate(node_peers):
        copy = remote(look_out.at[peer], look_in.at[me], look_send.at[k], look_recv.at[me], peer, mine)
        copy.start()
        sends.append(copy)
    look_in[pl.ds(me, 1)] = look_out[pl.ds(me, 1)]

    def piece(index, layer):
        return remote(
            proj.at[index, layer],
            proj.at[index, layer],
            proj_send.at[0],
            proj_recv.at[index, layer],
            2 * z + flip_y,
            mine,
        )

    for k, peer in enumerate(across):
        piece(peer, y).wait_recv()
        copy = remote(
            proj.at[peer, y],
            proj.at[peer, y],
            proj_send.at[3 + k],
            proj_recv.at[peer, y],
            2 * z + flip_y,
            mine,
        )
        copy.start()
        sends.append(copy)
    for peer in node_peers:
        remote(look_in.at[peer], look_in.at[peer], look_send.at[0], look_recv.at[peer], peer, mine).wait_recv()

    row = lax.broadcasted_iota(jnp.int32, (slots, nodes * 8), 0)
    col = lax.broadcasted_iota(jnp.int32, (slots, nodes * 8), 1)
    block = owner_of(row)
    pack = (col == block * 8 + (row - block * caps)).astype(F32).astype(BF16)
    own_front = matmul(pack, look_in[...].reshape(nodes * 8, look_in.shape[2]).astype(BF16))
    front[pl.ds(mine, 1)] = own_front.astype(BF16)[None]
    in_order[pl.ds(me, 1)] = own_front.astype(BF16)[None]
    for k, peer in enumerate(feat_peers):
        copy = remote(front.at[mine], front.at[mine], front_send.at[k], front_recv.at[mine], me, peer)
        copy.start()
        sends.append(copy)

    for k, peer in enumerate(node_peers):
        copy = remote(
            front.at[mine], in_order.at[me], order_send.at[k], order_recv.at[me], peer, mine
        )
        copy.start()
        sends.append(copy)

    loads[6].wait()
    preact_ref[...] = jnp.zeros_like(preact_ref)

    @pl.loop(0, feats)
    def _(k):
        index = 2 * lax.rem(x + k // 2, 2) + lax.rem(core + lax.rem(k, 2), 2)

        @pl.when(k > 0)
        def _():
            remote(front.at[index], front.at[index], front_send.at[0], front_recv.at[index], me, index).wait_recv()

        @pl.when(k == 1)
        def _():
            remote(proj.at[index], proj.at[index], proj_send.at[0], proj_recv.at[index, 0], me, index).wait_recv()

        @pl.when(k > 1)
        def _():
            piece(index, flip_y).wait_recv()

        held = front[pl.ds(index, 1)][0]
        own_rows = matmul(chosen_rows, held).astype(BF16)
        averaged = (matmul(tally_rows, held) * share_rows).astype(BF16)
        weight = proj[pl.ds(index, 1)][0]
        preact_ref[...] += matmul(own_rows, weight[0]) + matmul(averaged, weight[1])

    preact = preact_ref[...]
    square = preact * preact
    bent = jnp.tanh(0.7978845608 * (preact + 0.044715 * preact * square))
    rise = 0.7978845608 * (1.0 + 3.0 * 0.044715 * square)
    half = 0.5 * (1.0 + bent)
    loads[7].wait()
    slope = upstream[...].astype(F32) * (half + 0.5 * preact * (1.0 - bent * bent) * rise)
    both = matmul(back, slope.astype(BF16))
    own_terms[0] = both[:slots].astype(BF16)
    own_terms[1] = (both[slots : 2 * slots] + both[2 * slots :]).astype(BF16)
    keep = pltpu.make_async_copy(own_terms, terms.at[mine, me], local_sem.at[8])
    keep.start()

    if depth == 4:
        half_z, turned = z // 2, z // 2 + z % 2 - 2 * (z // 2) * (z % 2)
        depths = [z] + [
            near + half_z * (3 - 2 * near) for near in (1 - turned, 2, 3)
        ]
    else:
        depths = [z] + [lax.rem(z + k, depth) for k in range(1, depth)]
    counter = [0]

    def pass_on(node, feat, to_node, to_feat, src=None):
        copy = remote(
            terms.at[feat, node] if src is None else src,
            terms.at[feat, node],
            term_send.at[counter[0]],
            term_recv.at[feat, node],
            to_node,
            to_feat,
        )
        counter[0] += 1
        copy.start()
        sends.append(copy)

    def arrived(node, feat):
        remote(
            terms.at[feat, node],
            terms.at[feat, node],
            term_send.at[0],
            term_recv.at[feat, node],
            me,
            2 * x + flip_core,
        ).wait_recv()

    to_y = (2 * z + flip_y, mine)
    to_x = (me, 2 * flip_x + core)
    to_core = (me, 2 * x + flip_core)
    def spread(k):
        for target in (to_y, to_x, to_core):
            pass_on(2 * depths[k] + y, mine, *target, src=own_terms if k == 0 else None)

    for k in range(1, depth):
        pass_on(me, mine, 2 * depths[k] + y, mine, own_terms)
    spread(0)

    hid_out[...] = (preact * half).astype(BF16)

    def out_rows(index):
        return hid_out.at[pl.ds(pl.multiple_of(index * portion, portion), portion), :]

    for k, peer in enumerate(feat_peers):
        copy = remote(out_rows(peer), hidden_ref.at[mine], hid_send.at[k], hid_recv.at[mine], me, peer)
        copy.start()
        sends.append(copy)
    keep_rows = pltpu.make_async_copy(out_rows(mine), hidden_ref.at[mine], local_sem.at[9])
    keep_rows.start()

    for peer in node_peers:
        remote(in_order.at[peer], in_order.at[peer], order_send.at[0], order_recv.at[peer], peer, mine).wait_recv()
    ordered_ref[...] = in_order[...].reshape(nodes * slots, in_order.shape[2]).T

    across = across[0]
    early = 1

    def turn(k):
        node_y, node_x = 2 * depths[k] + flip_y, 2 * depths[k] + y
        arrived(node_y, mine)
        if k < early:
            pass_on(node_y, mine, *to_x)
        pass_on(node_y, mine, *to_core)
        arrived(node_x, across)
        if k >= early:
            pass_on(node_x, across, *to_y)
        pass_on(node_x, across, *to_core)

    for k in range(1, depth):
        arrived(2 * depths[k] + y, mine)
        spread(k)
        turn(k - 1)
    turn(depth - 1)

    for k in range(depth):
        node = 2 * depths[k] + flip_y
        arrived(node, across)
        pass_on(node, across, *to_core)
    for feat in (2 * x + flip_core, 2 * flip_x + flip_core):
        for node in range(nodes):
            arrived(node, feat)
    for peer in feat_peers:
        remote(hidden_ref.at[peer], hidden_ref.at[peer], hid_send.at[0], hid_recv.at[peer], me, peer).wait_recv()
    for copy in sends:
        copy.wait_send()
    keep.wait()
    keep_rows.wait()


def gradient_kernel(hidden_in, terms, ordered, hidden_ref, grad_ref, rows_out, grad, out_sem):
    feats, nodes, layers, slots, width = terms.shape
    for k in range(feats):
        rows_out[:, k * width : (k + 1) * width] = hidden_in[k]
    keep_rows = pltpu.make_async_copy(rows_out, hidden_ref, out_sem.at[feats])
    keep_rows.start()

    def part(feat):
        columns = pl.ds(pl.multiple_of(feat * width, width), width)
        return pltpu.make_async_copy(grad.at[feat], grad_ref.at[:, :, columns], out_sem.at[feat])

    @pl.loop(0, feats)
    def _(feat):
        held = terms[pl.ds(feat, 1)][0]
        for layer in range(layers):
            total = matmul(ordered[...], held[:, layer].reshape(nodes * slots, width))
            grad[pl.ds(feat, 1), layer : layer + 1] = total[None, None]
        part(feat).start()

    @pl.loop(0, feats)
    def _(feat):
        part(feat).wait()

    keep_rows.wait()


def compact_step(
    feature_table,
    weights,
    request_rows,
    request_counts,
    neighbors,
    nbr_counts,
    self_rows,
    grad_hidden,
):
    nodes, feats = lax.axis_size("node"), lax.axis_size("feat")
    caps, fan = request_rows.shape[2], neighbors.shape[1]
    slots = nodes * caps
    targets, hidden = grad_hidden.shape
    rows, features = feature_table.shape
    width, portion = hidden // feats, targets // feats
    dma = pltpu.SemaphoreType.DMA
    vmem = pl.BlockSpec(memory_space=pltpu.VMEM)
    anywhere = pl.BlockSpec(memory_space=pl.ANY)
    moves = nodes * feats - 1
    hidden_in, terms, ordered = pl.pallas_call(
        functools.partial(step_kernel, (nodes, feats, caps, fan)),
        out_shape=(
            jax.ShapeDtypeStruct((feats, portion, width), BF16),
            jax.ShapeDtypeStruct((feats, nodes, 2, slots, width), BF16),
            jax.ShapeDtypeStruct((features, nodes * slots), BF16),
        ),
        in_specs=[pl.BlockSpec(memory_space=pltpu.HBM)] * 8,
        out_specs=(anywhere, anywhere, vmem),
        scratch_shapes=[
            pltpu.VMEM((caps, 1, nodes), jnp.int32),
            pltpu.VMEM((1, nodes), jnp.int32),
            pltpu.VMEM((fan, targets), jnp.int32),
            pltpu.VMEM((1, targets), jnp.int32),
            pltpu.VMEM((1, targets), jnp.int32),
            pltpu.VMEM((features, rows), BF16),
            pltpu.VMEM((targets, width), BF16),
            pltpu.VMEM((8, 128), jnp.int32),
            pltpu.VMEM((nodes, 8, 128), jnp.int32),
            pltpu.VMEM((nodes, 8, features), F32),
            pltpu.VMEM((nodes, 8, features), F32),
            pltpu.VMEM((feats, slots, features), BF16),
            pltpu.VMEM((feats, 2, features, width), BF16),
            pltpu.VMEM((targets, width), F32),
            pltpu.VMEM((targets, width), BF16),
            pltpu.VMEM((2, slots, width), BF16),
            pltpu.VMEM((nodes, slots, features), BF16),
            dma((10,)),
            dma((nodes,)),
            dma((nodes,)),
            dma((nodes,)),
            dma((nodes,)),
            dma((feats,)),
            dma((feats,)),
            dma((nodes,)),
            dma((nodes,)),
            dma((5,)),
            dma((feats, 2)),
            dma((feats,)),
            dma((feats,)),
            dma((moves,)),
            dma((feats, nodes)),
        ],
        compiler_params=pltpu.CompilerParams(
            collective_id=0, has_side_effects=True, vmem_limit_bytes=24 * 1024 * 1024
        ),
    )(
        *(
            pltpu.with_memory_space_constraint(operand, pltpu.HBM)
            for operand in (
                request_rows.transpose(2, 0, 1),
                request_counts,
                neighbors.T,
                nbr_counts[None],
                self_rows[None],
                feature_table.T,
                weights,
                grad_hidden,
            )
        )
    )
    hbm = pl.BlockSpec(memory_space=pltpu.HBM)
    return pl.pallas_call(
        gradient_kernel,
        out_shape=(
            jax.ShapeDtypeStruct((portion, hidden), BF16),
            jax.ShapeDtypeStruct((2, features, hidden), F32),
        ),
        in_specs=[vmem, vmem, vmem],
        out_specs=(hbm, hbm),
        scratch_shapes=[
            pltpu.VMEM((portion, hidden), BF16),
            pltpu.VMEM((feats, 2, features, width), F32),
            dma((feats + 1,)),
        ],
        compiler_params=pltpu.CompilerParams(vmem_limit_bytes=24 * 1024 * 1024),
    )(hidden_in, terms, ordered)


def smooth_gate(values):
    return (
        0.5
        * values
        * (1.0 + jnp.tanh(0.7978845608 * (values + 0.044715 * values * values * values)))
    )


def activate(preact, upstream):
    output, pullback = jax.vjp(smooth_gate, preact)
    slope = pullback(upstream.astype(jnp.float32))[0]
    return (output.astype(jnp.bfloat16), slope.astype(jnp.bfloat16))


def aggregate(frontier, local_nbrs, local_counts):
    picked = frontier[local_nbrs]
    within = jnp.arange(local_nbrs.shape[1], dtype=jnp.int32)[None, :] < local_counts[:, None]
    summed = jnp.sum(
        jnp.where(within[:, :, None], picked, jnp.zeros_like(picked)), axis=1, dtype=jnp.float32
    )
    return (summed / local_counts[:, None].astype(jnp.float32)).astype(jnp.bfloat16)


def project(own_rows, averaged, weights):
    first = jnp.dot(own_rows, weights[0], preferred_element_type=jnp.float32)
    return first + jnp.dot(averaged, weights[1], preferred_element_type=jnp.float32)


def contract(left_side, right_side):
    return lax.dot_general(
        left_side, right_side, (((0,), (0,)), ((), ())), preferred_element_type=jnp.float32
    )


def per_device(
    feature_table,
    weights,
    request_rows,
    request_counts,
    neighbors,
    nbr_counts,
    self_rows,
    grad_hidden,
):
    slot_count = request_rows.shape[2]
    looked = feature_table[
        lax.all_to_all(request_rows[0], "node", split_axis=0, concat_axis=0, tiled=True)
    ]
    fetched = lax.all_to_all(looked, "node", split_axis=0, concat_axis=0, tiled=True)
    filled = jnp.arange(slot_count, dtype=jnp.int32)[None, :] < request_counts[0][:, None]
    frontier = jnp.where(filled[:, :, None], fetched, jnp.zeros_like(fetched)).reshape(
        -1, fetched.shape[2]
    )
    own_rows = frontier[self_rows]
    averaged = aggregate(frontier, neighbors, nbr_counts)
    groups = lax.axis_size("feat")
    portion = own_rows.shape[0] // groups
    preact = lax.psum(project(own_rows, averaged, weights), "feat")
    output_all, slope = activate(preact, grad_hidden)
    hidden = lax.dynamic_slice_in_dim(output_all, lax.axis_index("feat") * portion, portion, 0)
    grad_terms = jnp.stack([contract(own_rows, slope), contract(averaged, slope)])
    weight_grad = lax.psum(grad_terms, "node")
    return (hidden, weight_grad)


def solution(mesh):
    placed = (
        P("node", "feat"),
        P(None, "feat", None),
        P("node", None, None),
        P("node", None),
        P("node", None),
        P("node"),
        P("node"),
        P("node", None),
    )
    nodes, feats = mesh.shape["node"], mesh.shape["feat"]

    def per_slice(feature_table, weights, request_rows, *others):
        slots = nodes * request_rows.shape[2]
        plan = per_device
        if feats == 4 and nodes % 2 == 0 and slots % 16 == 0 and slots <= 128 and request_rows.shape[2] <= 8:
            plan = compact_step
        return plan(feature_table, weights, request_rows, *others)

    return jax.shard_map(
        per_slice,
        mesh=mesh,
        in_specs=placed,
        out_specs=(P(("node", "feat"), None), P(None, "feat", None)),
        check_vma=False,
    )
```

```python
import functools

import jax
import jax.numpy as jnp
from jax import lax
from jax.experimental import pallas as pl
from jax.experimental.pallas import tpu as pltpu
from jax.sharding import PartitionSpec as P

MESH = pl.DeviceIdType.MESH
F32, BF16 = jnp.float32, jnp.bfloat16


def matmul(left, right):
    return jnp.dot(left, right, preferred_element_type=F32)


def step_kernel(
    sizes,
    request_ref,
    counts_ref,
    nbrs_ref,
    nbr_counts_ref,
    self_ref,
    table_ref,
    weights_ref,
    upstream_ref,
    hidden_ref,
    terms,
    ordered_ref,
    request,
    counts,
    nbrs,
    nbr_counts,
    self_rows,
    table,
    upstream,
    ask_out,
    asked,
    look_out,
    look_in,
    front,
    proj,
    preact_ref,
    hid_out,
    own_terms,
    in_order,
    local_sem,
    ask_send,
    ask_recv,
    look_send,
    look_recv,
    front_send,
    front_recv,
    order_send,
    order_recv,
    proj_send,
    proj_recv,
    hid_send,
    hid_recv,
    term_send,
    term_recv,
):
    nodes, feats, caps, fan = sizes
    slots = nodes * caps
    depth = nodes // 2
    portion = hidden_ref.shape[1]
    width = hidden_ref.shape[2]
    me, mine = lax.axis_index("node"), lax.axis_index("feat")
    z, y, x, core = me // 2, me % 2, mine // 2, mine % 2
    node_peers = [lax.rem(me + k, nodes) for k in range(1, nodes)]
    feat_peers = [lax.rem(mine + k, feats) for k in range(1, feats)]
    my_columns = pl.ds(pl.multiple_of(mine * width, width), width)

    def columns(index):
        return pl.ds(pl.multiple_of(index * width, width), width)

    def remote(src, dst, send, recv, node, feat):
        return pltpu.make_async_remote_copy(
            src_ref=src,
            dst_ref=dst,
            send_sem=send,
            recv_sem=recv,
            device_id=(node, feat),
            device_id_type=MESH,
        )

    loads = []
    for k, (src, dst) in enumerate(
        (
            (request_ref, request),
            (nbrs_ref, nbrs),
            (nbr_counts_ref, nbr_counts),
            (self_ref, self_rows),
            (counts_ref, counts),
            (table_ref, table),
            (weights_ref.at[:, :, my_columns], proj.at[mine]),
            (upstream_ref.at[:, my_columns], upstream),
        )
    ):
        copy = pltpu.make_async_copy(src, dst, local_sem.at[k])
        copy.start()
        loads.append(copy)

    barrier = pltpu.get_barrier_semaphore()
    for peer in node_peers:
        pl.semaphore_signal(barrier, inc=1, device_id=(peer, mine), device_id_type=MESH)
    for peer in feat_peers:
        pl.semaphore_signal(barrier, inc=1, device_id=(me, peer), device_id_type=MESH)

    ask_out[...] = jnp.zeros_like(ask_out)
    loads[0].wait()
    for k in range(caps):
        ask_out[k : k + 1, 0:nodes] = request[k]
    pl.semaphore_wait(barrier, nodes + feats - 2)

    sends = []
    for k, peer in enumerate(node_peers):
        copy = remote(ask_out, asked.at[me], ask_send.at[k], ask_recv.at[me], peer, mine)
        copy.start()
        sends.append(copy)
    flip_y, flip_x, flip_core = 1 - y, 1 - x, 1 - core
    sibling = 2 * x + flip_core
    across = (2 * flip_x + core, 2 * flip_x + flip_core)
    for k, peer in enumerate(across):
        copy = remote(
            weights_ref.at[y, :, columns(peer)],
            proj.at[mine, y],
            proj_send.at[k],
            proj_recv.at[mine, y],
            me,
            peer,
        )
        copy.start()
        sends.append(copy)
    copy = remote(
        weights_ref.at[:, :, columns(sibling)],
        proj.at[mine],
        proj_send.at[2],
        proj_recv.at[mine, 0],
        me,
        sibling,
    )
    copy.start()
    sends.append(copy)
    asked[pl.ds(me, 1)] = ask_out[...][None]

    for copy in loads[1:5]:
        copy.wait()
    targets = nbrs.shape[1]

    def owner_of(slot):
        owner = jnp.zeros_like(slot)
        for k in range(1, nodes):
            owner = owner + (slot >= k * caps).astype(jnp.int32)
        return owner

    held_by = owner_of(lax.broadcasted_iota(jnp.int32, (slots, nodes), 0))
    here = lax.broadcasted_iota(jnp.int32, (slots, nodes), 1) == held_by
    limit = jnp.sum(
        jnp.where(here, counts[...].astype(F32), 0.0), axis=1, keepdims=True
    )
    slot = lax.broadcasted_iota(jnp.int32, (slots, targets), 0)
    live = (slot - owner_of(slot) * caps).astype(F32) < limit
    chosen = jnp.where(live & (slot == self_rows[...]), 1.0, 0.0).astype(F32)
    valid = nbr_counts[...]
    tally = jnp.zeros((slots, targets), F32)
    for k in range(fan):
        tally = tally + jnp.where((slot == nbrs[k : k + 1, :]) & (valid > k), 1.0, 0.0)
    tally = jnp.where(live, tally, 0.0)
    share = 1.0 / valid.astype(F32)
    mean = tally * share
    mean_high = mean.astype(BF16)
    mean_low = (mean - mean_high.astype(F32)).astype(BF16)
    back = jnp.concatenate([chosen.astype(BF16), mean_high, mean_low], axis=0)
    chosen_rows = chosen.T.astype(BF16)
    tally_rows = tally.T.astype(BF16)
    share_rows = jnp.broadcast_to(share, (128, targets)).T[:, 0:1]

    for peer in node_peers:
        remote(asked.at[peer], asked.at[peer], ask_send.at[0], ask_recv.at[peer], peer, mine).wait_recv()
    numbers = asked[...].reshape(nodes * 8, 128).astype(F32)
    lane = lax.broadcasted_iota(jnp.int32, numbers.shape, 1)
    wanted = jnp.sum(jnp.where(lane == me, numbers, 0.0), axis=1, keepdims=True)
    wanted = wanted.astype(jnp.int32)
    rows = table.shape[1]
    pick = (lax.broadcasted_iota(jnp.int32, (nodes * 8, rows), 1) == wanted).astype(F32)
    loads[5].wait()
    found = lax.dot_general(
        pick.astype(BF16), table[...], (((1,), (1,)), ((), ())), preferred_element_type=F32
    )
    look_out[...] = found.reshape(look_out.shape)
    for k, peer in enumerate(node_peers):
        copy = remote(look_out.at[peer], look_in.at[me], look_send.at[k], look_recv.at[me], peer, mine)
        copy.start()
        sends.append(copy)
    look_in[pl.ds(me, 1)] = look_out[pl.ds(me, 1)]

    def piece(index, layer):
        return remote(
            proj.at[index, layer],
            proj.at[index, layer],
            proj_send.at[0],
            proj_recv.at[index, layer],
            2 * z + flip_y,
            mine,
        )

    def pass_along(k):
        peer = across[k]
        piece(peer, y).wait_recv()
        copy = remote(
            proj.at[peer, y],
            proj.at[peer, y],
            proj_send.at[3 + k],
            proj_recv.at[peer, y],
            2 * z + flip_y,
            mine,
        )
        copy.start()
        sends.append(copy)

    pass_along(0)
    for peer in node_peers:
        remote(look_in.at[peer], look_in.at[peer], look_send.at[0], look_recv.at[peer], peer, mine).wait_recv()

    row = lax.broadcasted_iota(jnp.int32, (slots, nodes * 8), 0)
    col = lax.broadcasted_iota(jnp.int32, (slots, nodes * 8), 1)
    block = owner_of(row)
    pack = (col == block * 8 + (row - block * caps)).astype(F32).astype(BF16)
    own_front = matmul(pack, look_in[...].reshape(nodes * 8, look_in.shape[2]).astype(BF16))
    front[pl.ds(mine, 1)] = own_front.astype(BF16)[None]
    in_order[pl.ds(me, 1)] = own_front.astype(BF16)[None]
    for k, peer in enumerate(feat_peers):
        copy = remote(front.at[mine], front.at[mine], front_send.at[k], front_recv.at[mine], me, peer)
        copy.start()
        sends.append(copy)

    for k, peer in enumerate(node_peers):
        copy = remote(
            front.at[mine], in_order.at[me], order_send.at[k], order_recv.at[me], peer, mine
        )
        copy.start()
        sends.append(copy)

    pass_along(1)
    loads[6].wait()
    preact_ref[...] = jnp.zeros_like(preact_ref)

    @pl.loop(0, feats)
    def _(k):
        index = 2 * lax.rem(x + k // 2, 2) + lax.rem(core + lax.rem(k, 2), 2)

        @pl.when(k > 0)
        def _():
            remote(front.at[index], front.at[index], front_send.at[0], front_recv.at[index], me, index).wait_recv()

        @pl.when(k == 1)
        def _():
            remote(proj.at[index], proj.at[index], proj_send.at[0], proj_recv.at[index, 0], me, index).wait_recv()

        @pl.when(k > 1)
        def _():
            piece(index, flip_y).wait_recv()

        held = front[pl.ds(index, 1)][0]
        own_rows = matmul(chosen_rows, held).astype(BF16)
        averaged = (matmul(tally_rows, held) * share_rows).astype(BF16)
        weight = proj[pl.ds(index, 1)][0]
        preact_ref[...] += matmul(own_rows, weight[0]) + matmul(averaged, weight[1])

    preact = preact_ref[...]
    square = preact * preact
    bent = jnp.tanh(0.7978845608 * (preact + 0.044715 * preact * square))
    rise = 0.7978845608 * (1.0 + 3.0 * 0.044715 * square)
    half = 0.5 * (1.0 + bent)
    loads[7].wait()
    slope = upstream[...].astype(F32) * (half + 0.5 * preact * (1.0 - bent * bent) * rise)
    both = matmul(back, slope.astype(BF16))
    own_terms[0] = both[:slots].astype(BF16)
    own_terms[1] = (both[slots : 2 * slots] + both[2 * slots :]).astype(BF16)
    keep = pltpu.make_async_copy(own_terms, terms.at[mine, me], local_sem.at[8])
    keep.start()

    if depth == 4:
        half_z, turned = z // 2, z // 2 + z % 2 - 2 * (z // 2) * (z % 2)
        depths = [z] + [
            near + half_z * (3 - 2 * near) for near in (1 - turned, 2, 3)
        ]
    else:
        depths = [z] + [lax.rem(z + k, depth) for k in range(1, depth)]
    passed = []

    def pass_on(node, feat, to_node, to_feat, src=None):
        copy = remote(
            terms.at[feat, node] if src is None else src,
            terms.at[feat, node],
            term_send.at[len(passed)],
            term_recv.at[feat, node],
            to_node,
            to_feat,
        )
        copy.start()
        passed.append(copy)

    def arrived(node, feat):
        remote(
            terms.at[feat, node],
            terms.at[feat, node],
            term_send.at[0],
            term_recv.at[feat, node],
            me,
            2 * x + flip_core,
        ).wait_recv()

    to_y = (2 * z + flip_y, mine)
    to_x = (me, 2 * flip_x + core)
    to_core = (me, 2 * x + flip_core)

    def spread(k):
        for target in (to_y, to_x, to_core):
            pass_on(2 * depths[k] + y, mine, *target, src=own_terms if k == 0 else None)

    for k in range(1, depth):
        pass_on(me, mine, 2 * depths[k] + y, mine, own_terms)
    spread(0)
    arrived(2 * depths[1] + y, mine)
    spread(1)

    hid_out[...] = (preact * half).astype(BF16)

    def out_rows(index):
        return hid_out.at[pl.ds(pl.multiple_of(index * portion, portion), portion), :]

    for k, peer in enumerate(feat_peers):
        copy = remote(out_rows(peer), hidden_ref.at[mine], hid_send.at[k], hid_recv.at[mine], me, peer)
        copy.start()
        sends.append(copy)
    keep_rows = pltpu.make_async_copy(out_rows(mine), hidden_ref.at[mine], local_sem.at[9])
    keep_rows.start()

    arrived(2 * depths[2] + y, mine)
    spread(2)

    for peer in node_peers:
        remote(in_order.at[peer], in_order.at[peer], order_send.at[0], order_recv.at[peer], peer, mine).wait_recv()
    ordered_ref[...] = in_order[...].reshape(nodes * slots, in_order.shape[2]).T
    for k in range(3, depth):
        arrived(2 * depths[k] + y, mine)
        spread(k)
    for copy in sends:
        copy.wait_send()

    across = across[0]
    early = depth // 2

    def turn(k):
        node_y, node_x = 2 * depths[k] + flip_y, 2 * depths[k] + y
        arrived(node_y, mine)
        if k < early:
            pass_on(node_y, mine, *to_x)
        pass_on(node_y, mine, *to_core)
        arrived(node_x, across)
        if k >= early:
            pass_on(node_x, across, *to_y)
        pass_on(node_x, across, *to_core)

    for k in range(depth):
        turn(k)
    for copy in passed[: 2 * depth]:
        copy.wait_send()

    for k in range(depth):
        node = 2 * depths[k] + flip_y
        arrived(node, across)
        pass_on(node, across, *to_core)
    for feat in (2 * x + flip_core, 2 * flip_x + flip_core):
        for node in range(nodes):
            arrived(node, feat)
    for peer in feat_peers:
        remote(hidden_ref.at[peer], hidden_ref.at[peer], hid_send.at[0], hid_recv.at[peer], me, peer).wait_recv()
    for copy in passed[2 * depth :]:
        copy.wait_send()
    keep.wait()
    keep_rows.wait()


def gradient_kernel(hidden_in, terms, ordered, hidden_ref, grad_ref, rows_out, grad, out_sem):
    feats, nodes, layers, slots, width = terms.shape
    for k in range(feats):
        rows_out[:, k * width : (k + 1) * width] = hidden_in[k]
    keep_rows = pltpu.make_async_copy(rows_out, hidden_ref, out_sem.at[feats])
    keep_rows.start()

    def part(feat):
        columns = pl.ds(pl.multiple_of(feat * width, width), width)
        return pltpu.make_async_copy(grad.at[feat], grad_ref.at[:, :, columns], out_sem.at[feat])

    @pl.loop(0, feats)
    def _(feat):
        held = terms[pl.ds(feat, 1)][0]
        for layer in range(layers):
            total = matmul(ordered[...], held[:, layer].reshape(nodes * slots, width))
            grad[pl.ds(feat, 1), layer : layer + 1] = total[None, None]
        part(feat).start()

    @pl.loop(0, feats)
    def _(feat):
        part(feat).wait()

    keep_rows.wait()


def compact_step(
    feature_table,
    weights,
    request_rows,
    request_counts,
    neighbors,
    nbr_counts,
    self_rows,
    grad_hidden,
):
    nodes, feats = lax.axis_size("node"), lax.axis_size("feat")
    caps, fan = request_rows.shape[2], neighbors.shape[1]
    slots = nodes * caps
    targets, hidden = grad_hidden.shape
    rows, features = feature_table.shape
    width, portion = hidden // feats, targets // feats
    dma = pltpu.SemaphoreType.DMA
    vmem = pl.BlockSpec(memory_space=pltpu.VMEM)
    anywhere = pl.BlockSpec(memory_space=pl.ANY)
    moves = nodes * feats - 1
    hidden_in, terms, ordered = pl.pallas_call(
        functools.partial(step_kernel, (nodes, feats, caps, fan)),
        out_shape=(
            jax.ShapeDtypeStruct((feats, portion, width), BF16),
            jax.ShapeDtypeStruct((feats, nodes, 2, slots, width), BF16),
            jax.ShapeDtypeStruct((features, nodes * slots), BF16),
        ),
        in_specs=[pl.BlockSpec(memory_space=pltpu.HBM)] * 8,
        out_specs=(anywhere, anywhere, vmem),
        scratch_shapes=[
            pltpu.VMEM((caps, 1, nodes), jnp.int32),
            pltpu.VMEM((1, nodes), jnp.int32),
            pltpu.VMEM((fan, targets), jnp.int32),
            pltpu.VMEM((1, targets), jnp.int32),
            pltpu.VMEM((1, targets), jnp.int32),
            pltpu.VMEM((features, rows), BF16),
            pltpu.VMEM((targets, width), BF16),
            pltpu.VMEM((8, 128), jnp.int32),
            pltpu.VMEM((nodes, 8, 128), jnp.int32),
            pltpu.VMEM((nodes, 8, features), F32),
            pltpu.VMEM((nodes, 8, features), F32),
            pltpu.VMEM((feats, slots, features), BF16),
            pltpu.VMEM((feats, 2, features, width), BF16),
            pltpu.VMEM((targets, width), F32),
            pltpu.VMEM((targets, width), BF16),
            pltpu.VMEM((2, slots, width), BF16),
            pltpu.VMEM((nodes, slots, features), BF16),
            dma((10,)),
            dma((nodes,)),
            dma((nodes,)),
            dma((nodes,)),
            dma((nodes,)),
            dma((feats,)),
            dma((feats,)),
            dma((nodes,)),
            dma((nodes,)),
            dma((5,)),
            dma((feats, 2)),
            dma((feats,)),
            dma((feats,)),
            dma((moves,)),
            dma((feats, nodes)),
        ],
        compiler_params=pltpu.CompilerParams(
            collective_id=0, has_side_effects=True, vmem_limit_bytes=24 * 1024 * 1024
        ),
    )(
        *(
            pltpu.with_memory_space_constraint(operand, pltpu.HBM)
            for operand in (
                request_rows.transpose(2, 0, 1),
                request_counts,
                neighbors.T,
                nbr_counts[None],
                self_rows[None],
                feature_table.T,
                weights,
                grad_hidden,
            )
        )
    )
    hbm = pl.BlockSpec(memory_space=pltpu.HBM)
    return pl.pallas_call(
        gradient_kernel,
        out_shape=(
            jax.ShapeDtypeStruct((portion, hidden), BF16),
            jax.ShapeDtypeStruct((2, features, hidden), F32),
        ),
        in_specs=[vmem, vmem, vmem],
        out_specs=(hbm, hbm),
        scratch_shapes=[
            pltpu.VMEM((portion, hidden), BF16),
            pltpu.VMEM((feats, 2, features, width), F32),
            dma((feats + 1,)),
        ],
        compiler_params=pltpu.CompilerParams(vmem_limit_bytes=24 * 1024 * 1024),
    )(hidden_in, terms, ordered)


def smooth_gate(values):
    return (
        0.5
        * values
        * (1.0 + jnp.tanh(0.7978845608 * (values + 0.044715 * values * values * values)))
    )


def activate(preact, upstream):
    output, pullback = jax.vjp(smooth_gate, preact)
    slope = pullback(upstream.astype(jnp.float32))[0]
    return (output.astype(jnp.bfloat16), slope.astype(jnp.bfloat16))


def aggregate(frontier, local_nbrs, local_counts):
    picked = frontier[local_nbrs]
    within = jnp.arange(local_nbrs.shape[1], dtype=jnp.int32)[None, :] < local_counts[:, None]
    summed = jnp.sum(
        jnp.where(within[:, :, None], picked, jnp.zeros_like(picked)), axis=1, dtype=jnp.float32
    )
    return (summed / local_counts[:, None].astype(jnp.float32)).astype(jnp.bfloat16)


def project(own_rows, averaged, weights):
    first = jnp.dot(own_rows, weights[0], preferred_element_type=jnp.float32)
    return first + jnp.dot(averaged, weights[1], preferred_element_type=jnp.float32)


def contract(left_side, right_side):
    return lax.dot_general(
        left_side, right_side, (((0,), (0,)), ((), ())), preferred_element_type=jnp.float32
    )


def per_device(
    feature_table,
    weights,
    request_rows,
    request_counts,
    neighbors,
    nbr_counts,
    self_rows,
    grad_hidden,
):
    slot_count = request_rows.shape[2]
    looked = feature_table[
        lax.all_to_all(request_rows[0], "node", split_axis=0, concat_axis=0, tiled=True)
    ]
    fetched = lax.all_to_all(looked, "node", split_axis=0, concat_axis=0, tiled=True)
    filled = jnp.arange(slot_count, dtype=jnp.int32)[None, :] < request_counts[0][:, None]
    frontier = jnp.where(filled[:, :, None], fetched, jnp.zeros_like(fetched)).reshape(
        -1, fetched.shape[2]
    )
    own_rows = frontier[self_rows]
    averaged = aggregate(frontier, neighbors, nbr_counts)
    groups = lax.axis_size("feat")
    portion = own_rows.shape[0] // groups
    preact = lax.psum(project(own_rows, averaged, weights), "feat")
    output_all, slope = activate(preact, grad_hidden)
    hidden = lax.dynamic_slice_in_dim(output_all, lax.axis_index("feat") * portion, portion, 0)
    grad_terms = jnp.stack([contract(own_rows, slope), contract(averaged, slope)])
    weight_grad = lax.psum(grad_terms, "node")
    return (hidden, weight_grad)


def solution(mesh):
    placed = (
        P("node", "feat"),
        P(None, "feat", None),
        P("node", None, None),
        P("node", None),
        P("node", None),
        P("node"),
        P("node"),
        P("node", None),
    )
    nodes, feats = mesh.shape["node"], mesh.shape["feat"]

    def per_slice(feature_table, weights, request_rows, *others):
        slots = nodes * request_rows.shape[2]
        plan = per_device
        if feats == 4 and nodes % 2 == 0 and nodes >= 6 and slots % 16 == 0 and slots <= 128 and request_rows.shape[2] <= 8:
            plan = compact_step
        return plan(feature_table, weights, request_rows, *others)

    return jax.shard_map(
        per_slice,
        mesh=mesh,
        in_specs=placed,
        out_specs=(P(("node", "feat"), None), P(None, "feat", None)),
        check_vma=False,
    )
```

```python
import functools

import jax
import jax.numpy as jnp
from jax import lax
from jax.experimental import pallas as pl
from jax.experimental.pallas import tpu as pltpu
from jax.sharding import PartitionSpec as P

MESH = pl.DeviceIdType.MESH
F32, BF16 = jnp.float32, jnp.bfloat16


def matmul(left, right):
    return jnp.dot(left, right, preferred_element_type=F32)


def step_kernel(
    sizes,
    request_ref,
    counts_ref,
    nbrs_ref,
    nbr_counts_ref,
    self_ref,
    table_ref,
    weights_ref,
    upstream_ref,
    hidden_ref,
    terms,
    ordered_ref,
    request,
    counts,
    nbrs,
    nbr_counts,
    self_rows,
    table,
    upstream,
    ask_out,
    asked,
    look_out,
    look_in,
    front,
    proj,
    part_out,
    part_in,
    hid_out,
    own_terms,
    in_order,
    local_sem,
    ask_send,
    ask_recv,
    look_send,
    look_recv,
    front_send,
    front_recv,
    order_send,
    order_recv,
    proj_send,
    proj_recv,
    part_send,
    part_recv,
    hid_send,
    hid_recv,
    term_send,
    term_recv,
):
    nodes, feats, caps, fan = sizes
    slots = nodes * caps
    depth = nodes // 2
    portion = hidden_ref.shape[1]
    width = hidden_ref.shape[2]
    me, mine = lax.axis_index("node"), lax.axis_index("feat")
    z, y, x, core = me // 2, me % 2, mine // 2, mine % 2
    node_peers = [lax.rem(me + k, nodes) for k in range(1, nodes)]
    feat_peers = [lax.rem(mine + k, feats) for k in range(1, feats)]
    my_columns = pl.ds(pl.multiple_of(mine * width, width), width)

    def columns(index):
        return pl.ds(pl.multiple_of(index * width, width), width)

    def remote(src, dst, send, recv, node, feat):
        return pltpu.make_async_remote_copy(
            src_ref=src,
            dst_ref=dst,
            send_sem=send,
            recv_sem=recv,
            device_id=(node, feat),
            device_id_type=MESH,
        )

    loads = []
    for k, (src, dst) in enumerate(
        (
            (request_ref, request),
            (nbrs_ref, nbrs),
            (nbr_counts_ref, nbr_counts),
            (self_ref, self_rows),
            (counts_ref, counts),
            (table_ref, table),
            (upstream_ref.at[:, my_columns], upstream),
            (weights_ref.at[:, :, columns(core)], proj.at[core, 0]),
            (weights_ref.at[:, :, columns(2 + core)], proj.at[core, 1]),
        )
    ):
        copy = pltpu.make_async_copy(src, dst, local_sem.at[k])
        copy.start()
        loads.append(copy)

    barrier = pltpu.get_barrier_semaphore()
    for peer in node_peers:
        pl.semaphore_signal(barrier, inc=1, device_id=(peer, mine), device_id_type=MESH)
    for peer in feat_peers:
        pl.semaphore_signal(barrier, inc=1, device_id=(me, peer), device_id_type=MESH)

    ask_out[...] = jnp.zeros_like(ask_out)
    loads[0].wait()
    for k in range(caps):
        ask_out[k : k + 1, 0:nodes] = request[k]
    pl.semaphore_wait(barrier, nodes + feats - 2)

    sends = []
    for k, peer in enumerate(node_peers):
        copy = remote(ask_out, asked.at[me], ask_send.at[k], ask_recv.at[me], peer, mine)
        copy.start()
        sends.append(copy)
    flip_y, flip_x, flip_core = 1 - y, 1 - x, 1 - core
    sibling = 2 * x + flip_core
    for half in range(2):
        copy = remote(
            weights_ref.at[:, :, columns(2 * half + flip_core)],
            proj.at[core, half],
            proj_send.at[half],
            proj_recv.at[half],
            me,
            sibling,
        )
        copy.start()
        sends.append(copy)
    asked[pl.ds(me, 1)] = ask_out[...][None]

    for copy in loads[1:5]:
        copy.wait()
    targets = nbrs.shape[1]

    def owner_of(slot):
        owner = jnp.zeros_like(slot)
        for k in range(1, nodes):
            owner = owner + (slot >= k * caps).astype(jnp.int32)
        return owner

    held_by = owner_of(lax.broadcasted_iota(jnp.int32, (slots, nodes), 0))
    here = lax.broadcasted_iota(jnp.int32, (slots, nodes), 1) == held_by
    limit = jnp.sum(
        jnp.where(here, counts[...].astype(F32), 0.0), axis=1, keepdims=True
    )
    slot = lax.broadcasted_iota(jnp.int32, (slots, targets), 0)
    live = (slot - owner_of(slot) * caps).astype(F32) < limit
    chosen = jnp.where(live & (slot == self_rows[...]), 1.0, 0.0).astype(F32)
    valid = nbr_counts[...]
    tally = jnp.zeros((slots, targets), F32)
    for k in range(fan):
        tally = tally + jnp.where((slot == nbrs[k : k + 1, :]) & (valid > k), 1.0, 0.0)
    tally = jnp.where(live, tally, 0.0)
    share = 1.0 / valid.astype(F32)
    mean = tally * share
    mean_high = mean.astype(BF16)
    mean_low = (mean - mean_high.astype(F32)).astype(BF16)
    back = jnp.concatenate([chosen.astype(BF16), mean_high, mean_low], axis=0)
    chosen_rows = chosen.T.astype(BF16)
    tally_rows = tally.T.astype(BF16)
    share_rows = jnp.broadcast_to(share, (128, targets)).T[:, 0:1]

    for peer in node_peers:
        remote(asked.at[peer], asked.at[peer], ask_send.at[0], ask_recv.at[peer], peer, mine).wait_recv()
    numbers = asked[...].reshape(nodes * 8, 128).astype(F32)
    lane = lax.broadcasted_iota(jnp.int32, numbers.shape, 1)
    wanted = jnp.sum(jnp.where(lane == me, numbers, 0.0), axis=1, keepdims=True)
    wanted = wanted.astype(jnp.int32)
    rows = table.shape[1]
    pick = (lax.broadcasted_iota(jnp.int32, (nodes * 8, rows), 1) == wanted).astype(F32)
    loads[5].wait()
    found = lax.dot_general(
        pick.astype(BF16), table[...], (((1,), (1,)), ((), ())), preferred_element_type=F32
    )
    look_out[...] = found.reshape(look_out.shape)
    for k, peer in enumerate(node_peers):
        copy = remote(look_out.at[peer], look_in.at[me], look_send.at[k], look_recv.at[me], peer, mine)
        copy.start()
        sends.append(copy)
    look_in[pl.ds(me, 1)] = look_out[pl.ds(me, 1)]

    for peer in node_peers:
        remote(look_in.at[peer], look_in.at[peer], look_send.at[0], look_recv.at[peer], peer, mine).wait_recv()

    row = lax.broadcasted_iota(jnp.int32, (slots, nodes * 8), 0)
    col = lax.broadcasted_iota(jnp.int32, (slots, nodes * 8), 1)
    block = owner_of(row)
    pack = (col == block * 8 + (row - block * caps)).astype(F32).astype(BF16)
    own_front = matmul(pack, look_in[...].reshape(nodes * 8, look_in.shape[2]).astype(BF16))
    front[pl.ds(core, 1)] = own_front.astype(BF16)[None]
    copy = remote(
        front.at[core], front.at[core], front_send.at[0], front_recv.at[0], me, sibling
    )
    copy.start()
    sends.append(copy)
    in_order[pl.ds(me, 1)] = own_front.astype(BF16)[None]
    for k, peer in enumerate(node_peers):
        copy = remote(
            front.at[core], in_order.at[me], order_send.at[k], order_recv.at[me], peer, mine
        )
        copy.start()
        sends.append(copy)

    for copy in loads[7:]:
        copy.wait()
    for half in range(2):
        remote(
            proj.at[flip_core, half], proj.at[flip_core, half], proj_send.at[half], proj_recv.at[half], me, sibling
        ).wait_recv()
    remote(
        front.at[flip_core], front.at[flip_core], front_send.at[0], front_recv.at[0], me, sibling
    ).wait_recv()

    def for_x(index):
        weight = [proj[pl.ds(k, 1), pl.ds(index, 1)][0, 0] for k in range(2)]
        return [
            matmul(front[0], weight[0][layer]) + matmul(front[1], weight[1][layer])
            for layer in range(2)
        ]

    away = for_x(flip_x)
    part_out[0] = away[0]
    part_out[1] = away[1]
    copy = remote(
        part_out, part_in, part_send.at[0], part_recv.at[0], me, 2 * flip_x + core
    )
    copy.start()
    sends.append(copy)
    kept = for_x(x)
    copy.wait_recv()

    def wide(rows_of, values):
        high = values.astype(BF16)
        low = (values - high.astype(F32)).astype(BF16)
        return matmul(rows_of, high) + matmul(rows_of, low)

    preact = wide(chosen_rows, kept[0] + part_in[0])
    preact = preact + wide(tally_rows, kept[1] + part_in[1]) * share_rows
    square = preact * preact
    bent = jnp.tanh(0.7978845608 * (preact + 0.044715 * preact * square))
    rise = 0.7978845608 * (1.0 + 3.0 * 0.044715 * square)
    half = 0.5 * (1.0 + bent)
    loads[6].wait()
    slope = upstream[...].astype(F32) * (half + 0.5 * preact * (1.0 - bent * bent) * rise)
    both = matmul(back, slope.astype(BF16))
    own_terms[0] = both[:slots].astype(BF16)
    own_terms[1] = (both[slots : 2 * slots] + both[2 * slots :]).astype(BF16)
    keep = pltpu.make_async_copy(own_terms, terms.at[mine, me], local_sem.at[9])
    keep.start()

    if depth == 4:
        half_z, turned = z // 2, z // 2 + z % 2 - 2 * (z // 2) * (z % 2)
        depths = [z] + [
            near + half_z * (3 - 2 * near) for near in (1 - turned, 2, 3)
        ]
    else:
        depths = [z] + [lax.rem(z + k, depth) for k in range(1, depth)]
    passed = []

    def pass_on(node, feat, to_node, to_feat, src=None):
        copy = remote(
            terms.at[feat, node] if src is None else src,
            terms.at[feat, node],
            term_send.at[len(passed)],
            term_recv.at[feat, node],
            to_node,
            to_feat,
        )
        copy.start()
        passed.append(copy)

    def arrived(node, feat):
        remote(
            terms.at[feat, node],
            terms.at[feat, node],
            term_send.at[0],
            term_recv.at[feat, node],
            me,
            2 * x + flip_core,
        ).wait_recv()

    to_y = (2 * z + flip_y, mine)
    to_x = (me, 2 * flip_x + core)
    to_core = (me, 2 * x + flip_core)

    def spread(k):
        for target in (to_y, to_x, to_core):
            pass_on(2 * depths[k] + y, mine, *target, src=own_terms if k == 0 else None)

    for k in range(1, depth):
        pass_on(me, mine, 2 * depths[k] + y, mine, own_terms)
    spread(0)
    arrived(2 * depths[1] + y, mine)
    spread(1)

    hid_out[...] = (preact * half).astype(BF16)

    def out_rows(index):
        return hid_out.at[pl.ds(pl.multiple_of(index * portion, portion), portion), :]

    for k, peer in enumerate(feat_peers):
        copy = remote(out_rows(peer), hidden_ref.at[mine], hid_send.at[k], hid_recv.at[mine], me, peer)
        copy.start()
        sends.append(copy)
    keep_rows = pltpu.make_async_copy(out_rows(mine), hidden_ref.at[mine], local_sem.at[10])
    keep_rows.start()

    arrived(2 * depths[2] + y, mine)
    spread(2)

    for peer in node_peers:
        remote(in_order.at[peer], in_order.at[peer], order_send.at[0], order_recv.at[peer], peer, mine).wait_recv()
    ordered_ref[...] = in_order[...].reshape(nodes * slots, in_order.shape[2]).T
    for k in range(3, depth):
        arrived(2 * depths[k] + y, mine)
        spread(k)
    for copy in sends:
        copy.wait_send()

    across = 2 * flip_x + core
    early = depth // 2

    def turn(k):
        node_y, node_x = 2 * depths[k] + flip_y, 2 * depths[k] + y
        arrived(node_y, mine)
        if k < early:
            pass_on(node_y, mine, *to_x)
        pass_on(node_y, mine, *to_core)
        arrived(node_x, across)
        if k >= early:
            pass_on(node_x, across, *to_y)
        pass_on(node_x, across, *to_core)

    for k in range(depth):
        turn(k)
    for copy in passed[: 2 * depth]:
        copy.wait_send()

    for k in range(depth):
        node = 2 * depths[k] + flip_y
        arrived(node, across)
        pass_on(node, across, *to_core)
    for feat in (2 * x + flip_core, 2 * flip_x + flip_core):
        for node in range(nodes):
            arrived(node, feat)
    for peer in feat_peers:
        remote(hidden_ref.at[peer], hidden_ref.at[peer], hid_send.at[0], hid_recv.at[peer], me, peer).wait_recv()
    for copy in passed[2 * depth :]:
        copy.wait_send()
    keep.wait()
    keep_rows.wait()


def gradient_kernel(hidden_in, terms, ordered, hidden_ref, grad_ref, rows_out, grad, out_sem):
    feats, nodes, layers, slots, width = terms.shape
    for k in range(feats):
        rows_out[:, k * width : (k + 1) * width] = hidden_in[k]
    keep_rows = pltpu.make_async_copy(rows_out, hidden_ref, out_sem.at[feats])
    keep_rows.start()

    def part(feat):
        columns = pl.ds(pl.multiple_of(feat * width, width), width)
        return pltpu.make_async_copy(grad.at[feat], grad_ref.at[:, :, columns], out_sem.at[feat])

    @pl.loop(0, feats)
    def _(feat):
        held = terms[pl.ds(feat, 1)][0]
        for layer in range(layers):
            total = matmul(ordered[...], held[:, layer].reshape(nodes * slots, width))
            grad[pl.ds(feat, 1), layer : layer + 1] = total[None, None]
        part(feat).start()

    @pl.loop(0, feats)
    def _(feat):
        part(feat).wait()

    keep_rows.wait()


def compact_step(
    feature_table,
    weights,
    request_rows,
    request_counts,
    neighbors,
    nbr_counts,
    self_rows,
    grad_hidden,
):
    nodes, feats = lax.axis_size("node"), lax.axis_size("feat")
    caps, fan = request_rows.shape[2], neighbors.shape[1]
    slots = nodes * caps
    targets, hidden = grad_hidden.shape
    rows, features = feature_table.shape
    width, portion = hidden // feats, targets // feats
    dma = pltpu.SemaphoreType.DMA
    vmem = pl.BlockSpec(memory_space=pltpu.VMEM)
    anywhere = pl.BlockSpec(memory_space=pl.ANY)
    moves = nodes * feats - 1
    hidden_in, terms, ordered = pl.pallas_call(
        functools.partial(step_kernel, (nodes, feats, caps, fan)),
        out_shape=(
            jax.ShapeDtypeStruct((feats, portion, width), BF16),
            jax.ShapeDtypeStruct((feats, nodes, 2, slots, width), BF16),
            jax.ShapeDtypeStruct((features, nodes * slots), BF16),
        ),
        in_specs=[pl.BlockSpec(memory_space=pltpu.HBM)] * 8,
        out_specs=(anywhere, anywhere, vmem),
        scratch_shapes=[
            pltpu.VMEM((caps, 1, nodes), jnp.int32),
            pltpu.VMEM((1, nodes), jnp.int32),
            pltpu.VMEM((fan, targets), jnp.int32),
            pltpu.VMEM((1, targets), jnp.int32),
            pltpu.VMEM((1, targets), jnp.int32),
            pltpu.VMEM((features, rows), BF16),
            pltpu.VMEM((targets, width), BF16),
            pltpu.VMEM((8, 128), jnp.int32),
            pltpu.VMEM((nodes, 8, 128), jnp.int32),
            pltpu.VMEM((nodes, 8, features), F32),
            pltpu.VMEM((nodes, 8, features), F32),
            pltpu.VMEM((2, slots, features), BF16),
            pltpu.VMEM((2, 2, 2, features, width), BF16),
            pltpu.VMEM((2, slots, width), F32),
            pltpu.VMEM((2, slots, width), F32),
            pltpu.VMEM((targets, width), BF16),
            pltpu.VMEM((2, slots, width), BF16),
            pltpu.VMEM((nodes, slots, features), BF16),
            dma((11,)),
            dma((nodes,)),
            dma((nodes,)),
            dma((nodes,)),
            dma((nodes,)),
            dma((1,)),
            dma((1,)),
            dma((nodes,)),
            dma((nodes,)),
            dma((2,)),
            dma((2,)),
            dma((1,)),
            dma((1,)),
            dma((feats,)),
            dma((feats,)),
            dma((moves,)),
            dma((feats, nodes)),
        ],
        compiler_params=pltpu.CompilerParams(
            collective_id=0, has_side_effects=True, vmem_limit_bytes=24 * 1024 * 1024
        ),
    )(
        *(
            pltpu.with_memory_space_constraint(operand, pltpu.HBM)
            for operand in (
                request_rows.transpose(2, 0, 1),
                request_counts,
                neighbors.T,
                nbr_counts[None],
                self_rows[None],
                feature_table.T,
                weights,
                grad_hidden,
            )
        )
    )
    hbm = pl.BlockSpec(memory_space=pltpu.HBM)
    return pl.pallas_call(
        gradient_kernel,
        out_shape=(
            jax.ShapeDtypeStruct((portion, hidden), BF16),
            jax.ShapeDtypeStruct((2, features, hidden), F32),
        ),
        in_specs=[vmem, vmem, vmem],
        out_specs=(hbm, hbm),
        scratch_shapes=[
            pltpu.VMEM((portion, hidden), BF16),
            pltpu.VMEM((feats, 2, features, width), F32),
            dma((feats + 1,)),
        ],
        compiler_params=pltpu.CompilerParams(vmem_limit_bytes=24 * 1024 * 1024),
    )(hidden_in, terms, ordered)


def smooth_gate(values):
    return (
        0.5
        * values
        * (1.0 + jnp.tanh(0.7978845608 * (values + 0.044715 * values * values * values)))
    )


def activate(preact, upstream):
    output, pullback = jax.vjp(smooth_gate, preact)
    slope = pullback(upstream.astype(jnp.float32))[0]
    return (output.astype(jnp.bfloat16), slope.astype(jnp.bfloat16))


def aggregate(frontier, local_nbrs, local_counts):
    picked = frontier[local_nbrs]
    within = jnp.arange(local_nbrs.shape[1], dtype=jnp.int32)[None, :] < local_counts[:, None]
    summed = jnp.sum(
        jnp.where(within[:, :, None], picked, jnp.zeros_like(picked)), axis=1, dtype=jnp.float32
    )
    return (summed / local_counts[:, None].astype(jnp.float32)).astype(jnp.bfloat16)


def project(own_rows, averaged, weights):
    first = jnp.dot(own_rows, weights[0], preferred_element_type=jnp.float32)
    return first + jnp.dot(averaged, weights[1], preferred_element_type=jnp.float32)


def contract(left_side, right_side):
    return lax.dot_general(
        left_side, right_side, (((0,), (0,)), ((), ())), preferred_element_type=jnp.float32
    )


def per_device(
    feature_table,
    weights,
    request_rows,
    request_counts,
    neighbors,
    nbr_counts,
    self_rows,
    grad_hidden,
):
    slot_count = request_rows.shape[2]
    looked = feature_table[
        lax.all_to_all(request_rows[0], "node", split_axis=0, concat_axis=0, tiled=True)
    ]
    fetched = lax.all_to_all(looked, "node", split_axis=0, concat_axis=0, tiled=True)
    filled = jnp.arange(slot_count, dtype=jnp.int32)[None, :] < request_counts[0][:, None]
    frontier = jnp.where(filled[:, :, None], fetched, jnp.zeros_like(fetched)).reshape(
        -1, fetched.shape[2]
    )
    own_rows = frontier[self_rows]
    averaged = aggregate(frontier, neighbors, nbr_counts)
    groups = lax.axis_size("feat")
    portion = own_rows.shape[0] // groups
    preact = lax.psum(project(own_rows, averaged, weights), "feat")
    output_all, slope = activate(preact, grad_hidden)
    hidden = lax.dynamic_slice_in_dim(output_all, lax.axis_index("feat") * portion, portion, 0)
    grad_terms = jnp.stack([contract(own_rows, slope), contract(averaged, slope)])
    weight_grad = lax.psum(grad_terms, "node")
    return (hidden, weight_grad)


def solution(mesh):
    placed = (
        P("node", "feat"),
        P(None, "feat", None),
        P("node", None, None),
        P("node", None),
        P("node", None),
        P("node"),
        P("node"),
        P("node", None),
    )
    nodes, feats = mesh.shape["node"], mesh.shape["feat"]

    def per_slice(feature_table, weights, request_rows, *others):
        slots = nodes * request_rows.shape[2]
        plan = per_device
        if feats == 4 and nodes % 2 == 0 and nodes >= 6 and slots % 16 == 0 and slots <= 128 and request_rows.shape[2] <= 8:
            plan = compact_step
        return plan(feature_table, weights, request_rows, *others)

    return jax.shard_map(
        per_slice,
        mesh=mesh,
        in_specs=placed,
        out_specs=(P(("node", "feat"), None), P(None, "feat", None)),
        check_vma=False,
    )
```

```python
import functools

import jax
import jax.numpy as jnp
from jax import lax
from jax.experimental import pallas as pl
from jax.experimental.pallas import tpu as pltpu
from jax.sharding import PartitionSpec as P

MESH = pl.DeviceIdType.MESH
F32, BF16 = jnp.float32, jnp.bfloat16


def matmul(left, right):
    return jnp.dot(left, right, preferred_element_type=F32)


def step_kernel(
    sizes,
    request_ref,
    counts_ref,
    nbrs_ref,
    nbr_counts_ref,
    self_ref,
    table_ref,
    weights_ref,
    upstream_ref,
    hidden_ref,
    terms,
    ordered_ref,
    request,
    counts,
    nbrs,
    nbr_counts,
    self_rows,
    table,
    upstream,
    ask_out,
    asked,
    look_out,
    look_in,
    front,
    proj,
    preact_ref,
    hid_out,
    own_terms,
    in_order,
    local_sem,
    ask_send,
    ask_recv,
    look_send,
    look_recv,
    front_send,
    front_recv,
    order_send,
    order_recv,
    proj_send,
    proj_recv,
    hid_send,
    hid_recv,
    term_send,
    term_recv,
):
    nodes, feats, caps, fan = sizes
    slots = nodes * caps
    depth = nodes // 2
    portion = hidden_ref.shape[1]
    width = hidden_ref.shape[2]
    me, mine = lax.axis_index("node"), lax.axis_index("feat")
    z, y, x, core = me // 2, me % 2, mine // 2, mine % 2
    node_peers = [lax.rem(me + k, nodes) for k in range(1, nodes)]
    feat_peers = [lax.rem(mine + k, feats) for k in range(1, feats)]
    my_columns = pl.ds(pl.multiple_of(mine * width, width), width)

    def columns(index):
        return pl.ds(pl.multiple_of(index * width, width), width)

    def remote(src, dst, send, recv, node, feat):
        return pltpu.make_async_remote_copy(
            src_ref=src,
            dst_ref=dst,
            send_sem=send,
            recv_sem=recv,
            device_id=(node, feat),
            device_id_type=MESH,
        )

    loads = []
    for k, (src, dst) in enumerate(
        (
            (request_ref, request),
            (nbrs_ref, nbrs),
            (nbr_counts_ref, nbr_counts),
            (self_ref, self_rows),
            (counts_ref, counts),
            (table_ref, table),
            (weights_ref.at[:, :, my_columns], proj.at[mine]),
            (upstream_ref.at[:, my_columns], upstream),
        )
    ):
        copy = pltpu.make_async_copy(src, dst, local_sem.at[k])
        copy.start()
        loads.append(copy)

    barrier = pltpu.get_barrier_semaphore()
    for peer in node_peers:
        pl.semaphore_signal(barrier, inc=1, device_id=(peer, mine), device_id_type=MESH)
    for peer in feat_peers:
        pl.semaphore_signal(barrier, inc=1, device_id=(me, peer), device_id_type=MESH)

    corner = (2 * z + 1 - y, 2 * (1 - x) + core)
    pl.semaphore_signal(barrier, inc=1, device_id=corner, device_id_type=MESH)
    ask_out[...] = jnp.zeros_like(ask_out)
    loads[0].wait()
    for k in range(caps):
        ask_out[k : k + 1, 0:nodes] = request[k]
    pl.semaphore_wait(barrier, nodes + feats - 1)

    sends = []
    for k, peer in enumerate(node_peers):
        copy = remote(ask_out, asked.at[me], ask_send.at[k], ask_recv.at[me], peer, mine)
        copy.start()
        sends.append(copy)
    flip_y, flip_x, flip_core = 1 - y, 1 - x, 1 - core
    sibling = 2 * x + flip_core
    across = (2 * flip_x + core, 2 * flip_x + flip_core)
    for k, peer in enumerate(across):
        copy = remote(
            weights_ref.at[y, :, columns(peer)],
            proj.at[mine, y],
            proj_send.at[k],
            proj_recv.at[mine, y],
            me,
            peer,
        )
        copy.start()
        sends.append(copy)
    copy = remote(
        weights_ref.at[:, :, columns(sibling)],
        proj.at[mine],
        proj_send.at[2],
        proj_recv.at[mine, 0],
        me,
        sibling,
    )
    copy.start()
    sends.append(copy)
    asked[pl.ds(me, 1)] = ask_out[...][None]

    for copy in loads[1:5]:
        copy.wait()
    targets = nbrs.shape[1]

    def owner_of(slot):
        owner = jnp.zeros_like(slot)
        for k in range(1, nodes):
            owner = owner + (slot >= k * caps).astype(jnp.int32)
        return owner

    held_by = owner_of(lax.broadcasted_iota(jnp.int32, (slots, nodes), 0))
    here = lax.broadcasted_iota(jnp.int32, (slots, nodes), 1) == held_by
    limit = jnp.sum(
        jnp.where(here, counts[...].astype(F32), 0.0), axis=1, keepdims=True
    )
    slot = lax.broadcasted_iota(jnp.int32, (slots, targets), 0)
    live = (slot - owner_of(slot) * caps).astype(F32) < limit
    chosen = jnp.where(live & (slot == self_rows[...]), 1.0, 0.0).astype(F32)
    valid = nbr_counts[...]
    tally = jnp.zeros((slots, targets), F32)
    for k in range(fan):
        tally = tally + jnp.where((slot == nbrs[k : k + 1, :]) & (valid > k), 1.0, 0.0)
    tally = jnp.where(live, tally, 0.0)
    share = 1.0 / valid.astype(F32)
    mean = tally * share
    mean_high = mean.astype(BF16)
    mean_low = (mean - mean_high.astype(F32)).astype(BF16)
    back = jnp.concatenate([chosen.astype(BF16), mean_high, mean_low], axis=0)
    chosen_rows = chosen.T.astype(BF16)
    tally_rows = tally.T.astype(BF16)
    share_rows = jnp.broadcast_to(share, (128, targets)).T[:, 0:1]

    for peer in node_peers:
        remote(asked.at[peer], asked.at[peer], ask_send.at[0], ask_recv.at[peer], peer, mine).wait_recv()
    numbers = asked[...].reshape(nodes * 8, 128).astype(F32)
    lane = lax.broadcasted_iota(jnp.int32, numbers.shape, 1)
    wanted = jnp.sum(jnp.where(lane == me, numbers, 0.0), axis=1, keepdims=True)
    wanted = wanted.astype(jnp.int32)
    rows = table.shape[1]
    pick = (lax.broadcasted_iota(jnp.int32, (nodes * 8, rows), 1) == wanted).astype(F32)
    loads[5].wait()
    found = lax.dot_general(
        pick.astype(BF16), table[...], (((1,), (1,)), ((), ())), preferred_element_type=F32
    )
    look_out[...] = found.reshape(look_out.shape)
    for k, peer in enumerate(node_peers):
        copy = remote(look_out.at[peer], look_in.at[me], look_send.at[k], look_recv.at[me], peer, mine)
        copy.start()
        sends.append(copy)
    look_in[pl.ds(me, 1)] = look_out[pl.ds(me, 1)]

    def piece(index, layer):
        return remote(
            proj.at[index, layer],
            proj.at[index, layer],
            proj_send.at[0],
            proj_recv.at[index, layer],
            2 * z + flip_y,
            mine,
        )

    def pass_along(k):
        peer = across[k]
        piece(peer, y).wait_recv()
        copy = remote(
            proj.at[peer, y],
            proj.at[peer, y],
            proj_send.at[3 + k],
            proj_recv.at[peer, y],
            2 * z + flip_y,
            mine,
        )
        copy.start()
        sends.append(copy)

    pass_along(0)
    pass_along(1)
    for peer in node_peers:
        remote(look_in.at[peer], look_in.at[peer], look_send.at[0], look_recv.at[peer], peer, mine).wait_recv()

    row = lax.broadcasted_iota(jnp.int32, (slots, nodes * 8), 0)
    col = lax.broadcasted_iota(jnp.int32, (slots, nodes * 8), 1)
    block = owner_of(row)
    pack = (col == block * 8 + (row - block * caps)).astype(F32).astype(BF16)
    own_front = matmul(pack, look_in[...].reshape(nodes * 8, look_in.shape[2]).astype(BF16))
    front[pl.ds(mine, 1)] = own_front.astype(BF16)[None]
    in_order[pl.ds(me, 1)] = own_front.astype(BF16)[None]
    for k, peer in enumerate(feat_peers):
        copy = remote(front.at[mine], front.at[mine], front_send.at[k], front_recv.at[mine], me, peer)
        copy.start()
        sends.append(copy)

    for k, peer in enumerate(node_peers):
        copy = remote(
            front.at[mine], in_order.at[me], order_send.at[k], order_recv.at[me], peer, mine
        )
        copy.start()
        sends.append(copy)

    loads[6].wait()
    preact_ref[...] = jnp.zeros_like(preact_ref)

    @pl.loop(0, feats)
    def _(k):
        index = 2 * lax.rem(x + k // 2, 2) + lax.rem(core + lax.rem(k, 2), 2)

        @pl.when(k > 0)
        def _():
            remote(front.at[index], front.at[index], front_send.at[0], front_recv.at[index], me, index).wait_recv()

        @pl.when(k == 1)
        def _():
            remote(proj.at[index], proj.at[index], proj_send.at[0], proj_recv.at[index, 0], me, index).wait_recv()

        @pl.when(k > 1)
        def _():
            piece(index, flip_y).wait_recv()

        held = front[pl.ds(index, 1)][0]
        own_rows = matmul(chosen_rows, held).astype(BF16)
        averaged = (matmul(tally_rows, held) * share_rows).astype(BF16)
        weight = proj[pl.ds(index, 1)][0]
        preact_ref[...] += matmul(own_rows, weight[0]) + matmul(averaged, weight[1])

    preact = preact_ref[...]
    square = preact * preact
    bent = jnp.tanh(0.7978845608 * (preact + 0.044715 * preact * square))
    rise = 0.7978845608 * (1.0 + 3.0 * 0.044715 * square)
    half = 0.5 * (1.0 + bent)
    loads[7].wait()
    slope = upstream[...].astype(F32) * (half + 0.5 * preact * (1.0 - bent * bent) * rise)
    both = matmul(back, slope.astype(BF16))
    own_terms[0] = both[:slots].astype(BF16)
    own_terms[1] = (both[slots : 2 * slots] + both[2 * slots :]).astype(BF16)
    keep = pltpu.make_async_copy(own_terms, terms.at[mine, me], local_sem.at[8])
    keep.start()

    if depth == 4:
        half_z, turned = z // 2, z // 2 + z % 2 - 2 * (z // 2) * (z % 2)
        depths = [z] + [
            near + half_z * (3 - 2 * near) for near in (1 - turned, 2, 3)
        ]
    else:
        depths = [z] + [lax.rem(z + k, depth) for k in range(1, depth)]
    passed = []

    def pass_on(node, feat, to_node, to_feat, src=None):
        copy = remote(
            terms.at[feat, node] if src is None else src,
            terms.at[feat, node],
            term_send.at[len(passed)],
            term_recv.at[feat, node],
            to_node,
            to_feat,
        )
        copy.start()
        passed.append(copy)

    def arrived(node, feat):
        remote(
            terms.at[feat, node],
            terms.at[feat, node],
            term_send.at[0],
            term_recv.at[feat, node],
            me,
            2 * x + flip_core,
        ).wait_recv()

    to_y = (2 * z + flip_y, mine)
    to_x = (me, 2 * flip_x + core)
    to_core = (me, 2 * x + flip_core)

    def spread(k):
        for target in (to_y, to_x, to_core):
            pass_on(2 * depths[k] + y, mine, *target, src=own_terms if k == 0 else None)
        if k >= 2:
            pass_on(2 * depths[k] + y, mine, *corner)

    for k in range(1, depth):
        pass_on(me, mine, 2 * depths[k] + y, mine, own_terms)
    spread(0)
    arrived(2 * depths[1] + y, mine)
    spread(1)

    hid_out[...] = (preact * half).astype(BF16)

    def out_rows(index):
        return hid_out.at[pl.ds(pl.multiple_of(index * portion, portion), portion), :]

    for k, peer in enumerate(feat_peers):
        copy = remote(out_rows(peer), hidden_ref.at[mine], hid_send.at[k], hid_recv.at[mine], me, peer)
        copy.start()
        sends.append(copy)
    keep_rows = pltpu.make_async_copy(out_rows(mine), hidden_ref.at[mine], local_sem.at[9])
    keep_rows.start()

    arrived(2 * depths[2] + y, mine)
    spread(2)

    for peer in node_peers:
        remote(in_order.at[peer], in_order.at[peer], order_send.at[0], order_recv.at[peer], peer, mine).wait_recv()
    ordered_ref[...] = in_order[...].reshape(nodes * slots, in_order.shape[2]).T
    for k in range(3, depth):
        arrived(2 * depths[k] + y, mine)
        spread(k)
    for copy in sends:
        copy.wait_send()

    across = across[0]

    def turn(k):
        node_y, node_x = 2 * depths[k] + flip_y, 2 * depths[k] + y
        arrived(node_y, mine)
        if k == 0:
            pass_on(node_y, mine, *to_x)
        pass_on(node_y, mine, *to_core)
        arrived(node_x, across)
        if k == 1:
            pass_on(node_x, across, *to_y)
        pass_on(node_x, across, *to_core)

    for k in range(depth):
        turn(k)
    for copy in passed[: 2 * depth]:
        copy.wait_send()

    for k in range(depth):
        node = 2 * depths[k] + flip_y
        arrived(node, across)
        pass_on(node, across, *to_core)
    for feat in (2 * x + flip_core, 2 * flip_x + flip_core):
        for node in range(nodes):
            arrived(node, feat)
    for peer in feat_peers:
        remote(hidden_ref.at[peer], hidden_ref.at[peer], hid_send.at[0], hid_recv.at[peer], me, peer).wait_recv()
    for copy in passed[2 * depth :]:
        copy.wait_send()
    keep.wait()
    keep_rows.wait()


def gradient_kernel(hidden_in, terms, ordered, hidden_ref, grad_ref, rows_out, grad, out_sem):
    feats, nodes, layers, slots, width = terms.shape
    for k in range(feats):
        rows_out[:, k * width : (k + 1) * width] = hidden_in[k]
    keep_rows = pltpu.make_async_copy(rows_out, hidden_ref, out_sem.at[feats])
    keep_rows.start()

    def part(feat):
        columns = pl.ds(pl.multiple_of(feat * width, width), width)
        return pltpu.make_async_copy(grad.at[feat], grad_ref.at[:, :, columns], out_sem.at[feat])

    @pl.loop(0, feats)
    def _(feat):
        held = terms[pl.ds(feat, 1)][0]
        for layer in range(layers):
            total = matmul(ordered[...], held[:, layer].reshape(nodes * slots, width))
            grad[pl.ds(feat, 1), layer : layer + 1] = total[None, None]
        part(feat).start()

    @pl.loop(0, feats)
    def _(feat):
        part(feat).wait()

    keep_rows.wait()


def compact_step(
    feature_table,
    weights,
    request_rows,
    request_counts,
    neighbors,
    nbr_counts,
    self_rows,
    grad_hidden,
):
    nodes, feats = lax.axis_size("node"), lax.axis_size("feat")
    caps, fan = request_rows.shape[2], neighbors.shape[1]
    slots = nodes * caps
    targets, hidden = grad_hidden.shape
    rows, features = feature_table.shape
    width, portion = hidden // feats, targets // feats
    dma = pltpu.SemaphoreType.DMA
    vmem = pl.BlockSpec(memory_space=pltpu.VMEM)
    anywhere = pl.BlockSpec(memory_space=pl.ANY)
    moves = nodes * feats - 1
    hidden_in, terms, ordered = pl.pallas_call(
        functools.partial(step_kernel, (nodes, feats, caps, fan)),
        out_shape=(
            jax.ShapeDtypeStruct((feats, portion, width), BF16),
            jax.ShapeDtypeStruct((feats, nodes, 2, slots, width), BF16),
            jax.ShapeDtypeStruct((features, nodes * slots), BF16),
        ),
        in_specs=[pl.BlockSpec(memory_space=pltpu.HBM)] * 8,
        out_specs=(anywhere, anywhere, vmem),
        scratch_shapes=[
            pltpu.VMEM((caps, 1, nodes), jnp.int32),
            pltpu.VMEM((1, nodes), jnp.int32),
            pltpu.VMEM((fan, targets), jnp.int32),
            pltpu.VMEM((1, targets), jnp.int32),
            pltpu.VMEM((1, targets), jnp.int32),
            pltpu.VMEM((features, rows), BF16),
            pltpu.VMEM((targets, width), BF16),
            pltpu.VMEM((8, 128), jnp.int32),
            pltpu.VMEM((nodes, 8, 128), jnp.int32),
            pltpu.VMEM((nodes, 8, features), F32),
            pltpu.VMEM((nodes, 8, features), F32),
            pltpu.VMEM((feats, slots, features), BF16),
            pltpu.VMEM((feats, 2, features, width), BF16),
            pltpu.VMEM((targets, width), F32),
            pltpu.VMEM((targets, width), BF16),
            pltpu.VMEM((2, slots, width), BF16),
            pltpu.VMEM((nodes, slots, features), BF16),
            dma((10,)),
            dma((nodes,)),
            dma((nodes,)),
            dma((nodes,)),
            dma((nodes,)),
            dma((feats,)),
            dma((feats,)),
            dma((nodes,)),
            dma((nodes,)),
            dma((5,)),
            dma((feats, 2)),
            dma((feats,)),
            dma((feats,)),
            dma((moves,)),
            dma((feats, nodes)),
        ],
        compiler_params=pltpu.CompilerParams(
            collective_id=0, has_side_effects=True, vmem_limit_bytes=24 * 1024 * 1024
        ),
    )(
        *(
            pltpu.with_memory_space_constraint(operand, pltpu.HBM)
            for operand in (
                request_rows.transpose(2, 0, 1),
                request_counts,
                neighbors.T,
                nbr_counts[None],
                self_rows[None],
                feature_table.T,
                weights,
                grad_hidden,
            )
        )
    )
    hbm = pl.BlockSpec(memory_space=pltpu.HBM)
    return pl.pallas_call(
        gradient_kernel,
        out_shape=(
            jax.ShapeDtypeStruct((portion, hidden), BF16),
            jax.ShapeDtypeStruct((2, features, hidden), F32),
        ),
        in_specs=[vmem, vmem, vmem],
        out_specs=(hbm, hbm),
        scratch_shapes=[
            pltpu.VMEM((portion, hidden), BF16),
            pltpu.VMEM((feats, 2, features, width), F32),
            dma((feats + 1,)),
        ],
        compiler_params=pltpu.CompilerParams(vmem_limit_bytes=24 * 1024 * 1024),
    )(hidden_in, terms, ordered)


def smooth_gate(values):
    return (
        0.5
        * values
        * (1.0 + jnp.tanh(0.7978845608 * (values + 0.044715 * values * values * values)))
    )


def activate(preact, upstream):
    output, pullback = jax.vjp(smooth_gate, preact)
    slope = pullback(upstream.astype(jnp.float32))[0]
    return (output.astype(jnp.bfloat16), slope.astype(jnp.bfloat16))


def aggregate(frontier, local_nbrs, local_counts):
    picked = frontier[local_nbrs]
    within = jnp.arange(local_nbrs.shape[1], dtype=jnp.int32)[None, :] < local_counts[:, None]
    summed = jnp.sum(
        jnp.where(within[:, :, None], picked, jnp.zeros_like(picked)), axis=1, dtype=jnp.float32
    )
    return (summed / local_counts[:, None].astype(jnp.float32)).astype(jnp.bfloat16)


def project(own_rows, averaged, weights):
    first = jnp.dot(own_rows, weights[0], preferred_element_type=jnp.float32)
    return first + jnp.dot(averaged, weights[1], preferred_element_type=jnp.float32)


def contract(left_side, right_side):
    return lax.dot_general(
        left_side, right_side, (((0,), (0,)), ((), ())), preferred_element_type=jnp.float32
    )


def per_device(
    feature_table,
    weights,
    request_rows,
    request_counts,
    neighbors,
    nbr_counts,
    self_rows,
    grad_hidden,
):
    slot_count = request_rows.shape[2]
    looked = feature_table[
        lax.all_to_all(request_rows[0], "node", split_axis=0, concat_axis=0, tiled=True)
    ]
    fetched = lax.all_to_all(looked, "node", split_axis=0, concat_axis=0, tiled=True)
    filled = jnp.arange(slot_count, dtype=jnp.int32)[None, :] < request_counts[0][:, None]
    frontier = jnp.where(filled[:, :, None], fetched, jnp.zeros_like(fetched)).reshape(
        -1, fetched.shape[2]
    )
    own_rows = frontier[self_rows]
    averaged = aggregate(frontier, neighbors, nbr_counts)
    groups = lax.axis_size("feat")
    portion = own_rows.shape[0] // groups
    preact = lax.psum(project(own_rows, averaged, weights), "feat")
    output_all, slope = activate(preact, grad_hidden)
    hidden = lax.dynamic_slice_in_dim(output_all, lax.axis_index("feat") * portion, portion, 0)
    grad_terms = jnp.stack([contract(own_rows, slope), contract(averaged, slope)])
    weight_grad = lax.psum(grad_terms, "node")
    return (hidden, weight_grad)


def solution(mesh):
    placed = (
        P("node", "feat"),
        P(None, "feat", None),
        P("node", None, None),
        P("node", None),
        P("node", None),
        P("node"),
        P("node"),
        P("node", None),
    )
    nodes, feats = mesh.shape["node"], mesh.shape["feat"]

    def per_slice(feature_table, weights, request_rows, *others):
        slots = nodes * request_rows.shape[2]
        plan = per_device
        if feats == 4 and nodes % 2 == 0 and nodes >= 6 and slots % 16 == 0 and slots <= 128 and request_rows.shape[2] <= 8:
            plan = compact_step
        return plan(feature_table, weights, request_rows, *others)

    return jax.shard_map(
        per_slice,
        mesh=mesh,
        in_specs=placed,
        out_specs=(P(("node", "feat"), None), P(None, "feat", None)),
        check_vma=False,
    )
```

```python
import functools

import jax
import jax.numpy as jnp
from jax import lax
from jax.experimental import pallas as pl
from jax.experimental.pallas import tpu as pltpu
from jax.sharding import PartitionSpec as P

MESH = pl.DeviceIdType.MESH
F32, BF16 = jnp.float32, jnp.bfloat16


def matmul(left, right):
    return jnp.dot(left, right, preferred_element_type=F32)


def step_kernel(
    sizes,
    request_ref,
    counts_ref,
    nbrs_ref,
    nbr_counts_ref,
    self_ref,
    table_ref,
    weights_ref,
    upstream_ref,
    hidden_ref,
    terms,
    ordered_ref,
    request,
    counts,
    nbrs,
    nbr_counts,
    self_rows,
    table,
    upstream,
    ask_out,
    asked,
    look_out,
    look_in,
    front,
    proj,
    preact_ref,
    hid_out,
    own_terms,
    in_order,
    local_sem,
    ask_send,
    ask_recv,
    look_send,
    look_recv,
    front_send,
    front_recv,
    order_send,
    order_recv,
    proj_send,
    proj_recv,
    hid_send,
    hid_recv,
    term_send,
    term_recv,
):
    nodes, feats, caps, fan = sizes
    slots = nodes * caps
    depth = nodes // 2
    portion = hidden_ref.shape[1]
    width = hidden_ref.shape[2]
    me, mine = lax.axis_index("node"), lax.axis_index("feat")
    z, y, x, core = me // 2, me % 2, mine // 2, mine % 2
    node_peers = [lax.rem(me + k, nodes) for k in range(1, nodes)]
    feat_peers = [lax.rem(mine + k, feats) for k in range(1, feats)]
    my_columns = pl.ds(pl.multiple_of(mine * width, width), width)

    def columns(index):
        return pl.ds(pl.multiple_of(index * width, width), width)

    def remote(src, dst, send, recv, node, feat):
        return pltpu.make_async_remote_copy(
            src_ref=src,
            dst_ref=dst,
            send_sem=send,
            recv_sem=recv,
            device_id=(node, feat),
            device_id_type=MESH,
        )

    loads = []
    for k, (src, dst) in enumerate(
        (
            (request_ref, request),
            (nbrs_ref, nbrs),
            (nbr_counts_ref, nbr_counts),
            (self_ref, self_rows),
            (counts_ref, counts),
            (table_ref, table),
            (weights_ref.at[:, :, my_columns], proj.at[mine]),
            (upstream_ref.at[:, my_columns], upstream),
        )
    ):
        copy = pltpu.make_async_copy(src, dst, local_sem.at[k])
        copy.start()
        loads.append(copy)

    barrier = pltpu.get_barrier_semaphore()
    for peer in node_peers:
        pl.semaphore_signal(barrier, inc=1, device_id=(peer, mine), device_id_type=MESH)
    for peer in feat_peers:
        pl.semaphore_signal(barrier, inc=1, device_id=(me, peer), device_id_type=MESH)

    corner = (2 * z + 1 - y, 2 * (1 - x) + core)
    pl.semaphore_signal(barrier, inc=1, device_id=corner, device_id_type=MESH)
    ask_out[...] = jnp.zeros_like(ask_out)
    loads[0].wait()
    for k in range(caps):
        ask_out[k : k + 1, 0:nodes] = request[k]
    pl.semaphore_wait(barrier, nodes + feats - 1)

    sends = []
    for k, peer in enumerate(node_peers):
        copy = remote(ask_out, asked.at[me], ask_send.at[k], ask_recv.at[me], peer, mine)
        copy.start()
        sends.append(copy)
    flip_y, flip_x, flip_core = 1 - y, 1 - x, 1 - core
    sibling = 2 * x + flip_core
    across = (2 * flip_x + core, 2 * flip_x + flip_core)
    for k, peer in enumerate(across):
        copy = remote(
            weights_ref.at[y, :, columns(peer)],
            proj.at[mine, y],
            proj_send.at[k],
            proj_recv.at[mine, y],
            me,
            peer,
        )
        copy.start()
        sends.append(copy)
    copy = remote(
        weights_ref.at[:, :, columns(sibling)],
        proj.at[mine],
        proj_send.at[2],
        proj_recv.at[mine, 0],
        me,
        sibling,
    )
    copy.start()
    sends.append(copy)
    asked[pl.ds(me, 1)] = ask_out[...][None]

    for copy in loads[1:5]:
        copy.wait()
    targets = nbrs.shape[1]

    def owner_of(slot):
        owner = jnp.zeros_like(slot)
        for k in range(1, nodes):
            owner = owner + (slot >= k * caps).astype(jnp.int32)
        return owner

    held_by = owner_of(lax.broadcasted_iota(jnp.int32, (slots, nodes), 0))
    here = lax.broadcasted_iota(jnp.int32, (slots, nodes), 1) == held_by
    limit = jnp.sum(
        jnp.where(here, counts[...].astype(F32), 0.0), axis=1, keepdims=True
    )
    slot = lax.broadcasted_iota(jnp.int32, (slots, targets), 0)
    live = (slot - owner_of(slot) * caps).astype(F32) < limit
    chosen = jnp.where(live & (slot == self_rows[...]), 1.0, 0.0).astype(F32)
    valid = nbr_counts[...]
    tally = jnp.zeros((slots, targets), F32)
    for k in range(fan):
        tally = tally + jnp.where((slot == nbrs[k : k + 1, :]) & (valid > k), 1.0, 0.0)
    tally = jnp.where(live, tally, 0.0)
    share = 1.0 / valid.astype(F32)
    mean = tally * share
    mean_high = mean.astype(BF16)
    mean_low = (mean - mean_high.astype(F32)).astype(BF16)
    back = jnp.concatenate([chosen.astype(BF16), mean_high, mean_low], axis=0)
    chosen_rows = chosen.T.astype(BF16)
    tally_rows = tally.T.astype(BF16)
    share_rows = jnp.broadcast_to(share, (128, targets)).T[:, 0:1]

    for peer in node_peers:
        remote(asked.at[peer], asked.at[peer], ask_send.at[0], ask_recv.at[peer], peer, mine).wait_recv()
    numbers = asked[...].reshape(nodes * 8, 128).astype(F32)
    lane = lax.broadcasted_iota(jnp.int32, numbers.shape, 1)
    wanted = jnp.sum(jnp.where(lane == me, numbers, 0.0), axis=1, keepdims=True)
    wanted = wanted.astype(jnp.int32)
    rows = table.shape[1]
    pick = (lax.broadcasted_iota(jnp.int32, (nodes * 8, rows), 1) == wanted).astype(F32)
    loads[5].wait()
    found = lax.dot_general(
        pick.astype(BF16), table[...], (((1,), (1,)), ((), ())), preferred_element_type=F32
    )
    look_out[...] = found.reshape(look_out.shape)
    for k, peer in enumerate(node_peers):
        copy = remote(look_out.at[peer], look_in.at[me], look_send.at[k], look_recv.at[me], peer, mine)
        copy.start()
        sends.append(copy)
    look_in[pl.ds(me, 1)] = look_out[pl.ds(me, 1)]

    def piece(index, layer):
        return remote(
            proj.at[index, layer],
            proj.at[index, layer],
            proj_send.at[0],
            proj_recv.at[index, layer],
            2 * z + flip_y,
            mine,
        )

    def pass_along(k):
        peer = across[k]
        piece(peer, y).wait_recv()
        copy = remote(
            proj.at[peer, y],
            proj.at[peer, y],
            proj_send.at[3 + k],
            proj_recv.at[peer, y],
            2 * z + flip_y,
            mine,
        )
        copy.start()
        sends.append(copy)

    pass_along(0)
    pass_along(1)
    for peer in node_peers:
        remote(look_in.at[peer], look_in.at[peer], look_send.at[0], look_recv.at[peer], peer, mine).wait_recv()

    row = lax.broadcasted_iota(jnp.int32, (slots, nodes * 8), 0)
    col = lax.broadcasted_iota(jnp.int32, (slots, nodes * 8), 1)
    block = owner_of(row)
    pack = (col == block * 8 + (row - block * caps)).astype(F32).astype(BF16)
    own_front = matmul(pack, look_in[...].reshape(nodes * 8, look_in.shape[2]).astype(BF16))
    front[pl.ds(mine, 1)] = own_front.astype(BF16)[None]
    in_order[pl.ds(me, 1)] = own_front.astype(BF16)[None]
    for k, peer in enumerate(feat_peers):
        copy = remote(front.at[mine], front.at[mine], front_send.at[k], front_recv.at[mine], me, peer)
        copy.start()
        sends.append(copy)

    for k, peer in enumerate(node_peers):
        copy = remote(
            front.at[mine], in_order.at[me], order_send.at[k], order_recv.at[me], peer, mine
        )
        copy.start()
        sends.append(copy)

    loads[6].wait()
    preact_ref[...] = jnp.zeros_like(preact_ref)

    @pl.loop(0, feats)
    def _(k):
        index = 2 * lax.rem(x + k // 2, 2) + lax.rem(core + lax.rem(k, 2), 2)

        @pl.when(k > 0)
        def _():
            remote(front.at[index], front.at[index], front_send.at[0], front_recv.at[index], me, index).wait_recv()

        @pl.when(k == 1)
        def _():
            remote(proj.at[index], proj.at[index], proj_send.at[0], proj_recv.at[index, 0], me, index).wait_recv()

        @pl.when(k > 1)
        def _():
            piece(index, flip_y).wait_recv()

        held = front[pl.ds(index, 1)][0]
        own_rows = matmul(chosen_rows, held).astype(BF16)
        averaged = (matmul(tally_rows, held) * share_rows).astype(BF16)
        weight = proj[pl.ds(index, 1)][0]
        preact_ref[...] += matmul(own_rows, weight[0]) + matmul(averaged, weight[1])

    preact = preact_ref[...]
    square = preact * preact
    bent = jnp.tanh(0.7978845608 * (preact + 0.044715 * preact * square))
    rise = 0.7978845608 * (1.0 + 3.0 * 0.044715 * square)
    half = 0.5 * (1.0 + bent)
    loads[7].wait()
    slope = upstream[...].astype(F32) * (half + 0.5 * preact * (1.0 - bent * bent) * rise)
    both = matmul(back, slope.astype(BF16))
    own_terms[0] = both[:slots].astype(BF16)
    own_terms[1] = (both[slots : 2 * slots] + both[2 * slots :]).astype(BF16)
    keep = pltpu.make_async_copy(own_terms, terms.at[mine, me], local_sem.at[8])
    keep.start()

    if depth == 4:
        half_z, turned = z // 2, z // 2 + z % 2 - 2 * (z // 2) * (z % 2)
        depths = [z] + [
            near + half_z * (3 - 2 * near) for near in (1 - turned, 2, 3)
        ]
    else:
        depths = [z] + [lax.rem(z + k, depth) for k in range(1, depth)]
    passed = []

    def pass_on(node, feat, to_node, to_feat, src=None):
        copy = remote(
            terms.at[feat, node] if src is None else src,
            terms.at[feat, node],
            term_send.at[len(passed)],
            term_recv.at[feat, node],
            to_node,
            to_feat,
        )
        copy.start()
        passed.append(copy)

    def arrived(node, feat):
        remote(
            terms.at[feat, node],
            terms.at[feat, node],
            term_send.at[0],
            term_recv.at[feat, node],
            me,
            2 * x + flip_core,
        ).wait_recv()

    to_y = (2 * z + flip_y, mine)
    to_x = (me, 2 * flip_x + core)
    to_core = (me, 2 * x + flip_core)

    def spread(k):
        for target in (to_y, to_x, to_core):
            pass_on(2 * depths[k] + y, mine, *target, src=own_terms if k == 0 else None)
        if k >= 1:
            pass_on(2 * depths[k] + y, mine, *corner)

    for k in range(1, depth):
        pass_on(me, mine, 2 * depths[k] + y, mine, own_terms)
    spread(0)
    arrived(2 * depths[1] + y, mine)
    spread(1)

    hid_out[...] = (preact * half).astype(BF16)

    def out_rows(index):
        return hid_out.at[pl.ds(pl.multiple_of(index * portion, portion), portion), :]

    for k, peer in enumerate(feat_peers):
        copy = remote(out_rows(peer), hidden_ref.at[mine], hid_send.at[k], hid_recv.at[mine], me, peer)
        copy.start()
        sends.append(copy)
    keep_rows = pltpu.make_async_copy(out_rows(mine), hidden_ref.at[mine], local_sem.at[9])
    keep_rows.start()

    arrived(2 * depths[2] + y, mine)
    spread(2)

    for peer in node_peers:
        remote(in_order.at[peer], in_order.at[peer], order_send.at[0], order_recv.at[peer], peer, mine).wait_recv()
    ordered_ref[...] = in_order[...].reshape(nodes * slots, in_order.shape[2]).T
    for k in range(3, depth):
        arrived(2 * depths[k] + y, mine)
        spread(k)
    for copy in sends:
        copy.wait_send()

    across = across[0]

    def turn(k):
        node_y, node_x = 2 * depths[k] + flip_y, 2 * depths[k] + y
        arrived(node_y, mine)
        if k == 0:
            pass_on(node_y, mine, *to_x)
        pass_on(node_y, mine, *to_core)
        arrived(node_x, across)
        pass_on(node_x, across, *to_core)

    for k in range(depth):
        turn(k)
    for copy in passed[: 2 * depth]:
        copy.wait_send()

    for k in range(depth):
        node = 2 * depths[k] + flip_y
        arrived(node, across)
        pass_on(node, across, *to_core)
    for feat in (2 * x + flip_core, 2 * flip_x + flip_core):
        for node in range(nodes):
            arrived(node, feat)
    for peer in feat_peers:
        remote(hidden_ref.at[peer], hidden_ref.at[peer], hid_send.at[0], hid_recv.at[peer], me, peer).wait_recv()
    for copy in passed[2 * depth :]:
        copy.wait_send()
    keep.wait()
    keep_rows.wait()


def gradient_kernel(hidden_in, terms, ordered, hidden_ref, grad_ref, rows_out, grad, out_sem):
    feats, nodes, layers, slots, width = terms.shape
    for k in range(feats):
        rows_out[:, k * width : (k + 1) * width] = hidden_in[k]
    keep_rows = pltpu.make_async_copy(rows_out, hidden_ref, out_sem.at[feats])
    keep_rows.start()

    def part(feat):
        columns = pl.ds(pl.multiple_of(feat * width, width), width)
        return pltpu.make_async_copy(grad.at[feat], grad_ref.at[:, :, columns], out_sem.at[feat])

    @pl.loop(0, feats)
    def _(feat):
        held = terms[pl.ds(feat, 1)][0]
        for layer in range(layers):
            total = matmul(ordered[...], held[:, layer].reshape(nodes * slots, width))
            grad[pl.ds(feat, 1), layer : layer + 1] = total[None, None]
        part(feat).start()

    @pl.loop(0, feats)
    def _(feat):
        part(feat).wait()

    keep_rows.wait()


def compact_step(
    feature_table,
    weights,
    request_rows,
    request_counts,
    neighbors,
    nbr_counts,
    self_rows,
    grad_hidden,
):
    nodes, feats = lax.axis_size("node"), lax.axis_size("feat")
    caps, fan = request_rows.shape[2], neighbors.shape[1]
    slots = nodes * caps
    targets, hidden = grad_hidden.shape
    rows, features = feature_table.shape
    width, portion = hidden // feats, targets // feats
    dma = pltpu.SemaphoreType.DMA
    vmem = pl.BlockSpec(memory_space=pltpu.VMEM)
    anywhere = pl.BlockSpec(memory_space=pl.ANY)
    moves = nodes * feats - 1
    hidden_in, terms, ordered = pl.pallas_call(
        functools.partial(step_kernel, (nodes, feats, caps, fan)),
        out_shape=(
            jax.ShapeDtypeStruct((feats, portion, width), BF16),
            jax.ShapeDtypeStruct((feats, nodes, 2, slots, width), BF16),
            jax.ShapeDtypeStruct((features, nodes * slots), BF16),
        ),
        in_specs=[pl.BlockSpec(memory_space=pltpu.HBM)] * 8,
        out_specs=(anywhere, anywhere, vmem),
        scratch_shapes=[
            pltpu.VMEM((caps, 1, nodes), jnp.int32),
            pltpu.VMEM((1, nodes), jnp.int32),
            pltpu.VMEM((fan, targets), jnp.int32),
            pltpu.VMEM((1, targets), jnp.int32),
            pltpu.VMEM((1, targets), jnp.int32),
            pltpu.VMEM((features, rows), BF16),
            pltpu.VMEM((targets, width), BF16),
            pltpu.VMEM((8, 128), jnp.int32),
            pltpu.VMEM((nodes, 8, 128), jnp.int32),
            pltpu.VMEM((nodes, 8, features), F32),
            pltpu.VMEM((nodes, 8, features), F32),
            pltpu.VMEM((feats, slots, features), BF16),
            pltpu.VMEM((feats, 2, features, width), BF16),
            pltpu.VMEM((targets, width), F32),
            pltpu.VMEM((targets, width), BF16),
            pltpu.VMEM((2, slots, width), BF16),
            pltpu.VMEM((nodes, slots, features), BF16),
            dma((10,)),
            dma((nodes,)),
            dma((nodes,)),
            dma((nodes,)),
            dma((nodes,)),
            dma((feats,)),
            dma((feats,)),
            dma((nodes,)),
            dma((nodes,)),
            dma((5,)),
            dma((feats, 2)),
            dma((feats,)),
            dma((feats,)),
            dma((moves,)),
            dma((feats, nodes)),
        ],
        compiler_params=pltpu.CompilerParams(
            collective_id=0, has_side_effects=True, vmem_limit_bytes=24 * 1024 * 1024
        ),
    )(
        *(
            pltpu.with_memory_space_constraint(operand, pltpu.HBM)
            for operand in (
                request_rows.transpose(2, 0, 1),
                request_counts,
                neighbors.T,
                nbr_counts[None],
                self_rows[None],
                feature_table.T,
                weights,
                grad_hidden,
            )
        )
    )
    hbm = pl.BlockSpec(memory_space=pltpu.HBM)
    return pl.pallas_call(
        gradient_kernel,
        out_shape=(
            jax.ShapeDtypeStruct((portion, hidden), BF16),
            jax.ShapeDtypeStruct((2, features, hidden), F32),
        ),
        in_specs=[vmem, vmem, vmem],
        out_specs=(hbm, hbm),
        scratch_shapes=[
            pltpu.VMEM((portion, hidden), BF16),
            pltpu.VMEM((feats, 2, features, width), F32),
            dma((feats + 1,)),
        ],
        compiler_params=pltpu.CompilerParams(vmem_limit_bytes=24 * 1024 * 1024),
    )(hidden_in, terms, ordered)


def smooth_gate(values):
    return (
        0.5
        * values
        * (1.0 + jnp.tanh(0.7978845608 * (values + 0.044715 * values * values * values)))
    )


def activate(preact, upstream):
    output, pullback = jax.vjp(smooth_gate, preact)
    slope = pullback(upstream.astype(jnp.float32))[0]
    return (output.astype(jnp.bfloat16), slope.astype(jnp.bfloat16))


def aggregate(frontier, local_nbrs, local_counts):
    picked = frontier[local_nbrs]
    within = jnp.arange(local_nbrs.shape[1], dtype=jnp.int32)[None, :] < local_counts[:, None]
    summed = jnp.sum(
        jnp.where(within[:, :, None], picked, jnp.zeros_like(picked)), axis=1, dtype=jnp.float32
    )
    return (summed / local_counts[:, None].astype(jnp.float32)).astype(jnp.bfloat16)


def project(own_rows, averaged, weights):
    first = jnp.dot(own_rows, weights[0], preferred_element_type=jnp.float32)
    return first + jnp.dot(averaged, weights[1], preferred_element_type=jnp.float32)


def contract(left_side, right_side):
    return lax.dot_general(
        left_side, right_side, (((0,), (0,)), ((), ())), preferred_element_type=jnp.float32
    )


def per_device(
    feature_table,
    weights,
    request_rows,
    request_counts,
    neighbors,
    nbr_counts,
    self_rows,
    grad_hidden,
):
    slot_count = request_rows.shape[2]
    looked = feature_table[
        lax.all_to_all(request_rows[0], "node", split_axis=0, concat_axis=0, tiled=True)
    ]
    fetched = lax.all_to_all(looked, "node", split_axis=0, concat_axis=0, tiled=True)
    filled = jnp.arange(slot_count, dtype=jnp.int32)[None, :] < request_counts[0][:, None]
    frontier = jnp.where(filled[:, :, None], fetched, jnp.zeros_like(fetched)).reshape(
        -1, fetched.shape[2]
    )
    own_rows = frontier[self_rows]
    averaged = aggregate(frontier, neighbors, nbr_counts)
    groups = lax.axis_size("feat")
    portion = own_rows.shape[0] // groups
    preact = lax.psum(project(own_rows, averaged, weights), "feat")
    output_all, slope = activate(preact, grad_hidden)
    hidden = lax.dynamic_slice_in_dim(output_all, lax.axis_index("feat") * portion, portion, 0)
    grad_terms = jnp.stack([contract(own_rows, slope), contract(averaged, slope)])
    weight_grad = lax.psum(grad_terms, "node")
    return (hidden, weight_grad)


def solution(mesh):
    placed = (
        P("node", "feat"),
        P(None, "feat", None),
        P("node", None, None),
        P("node", None),
        P("node", None),
        P("node"),
        P("node"),
        P("node", None),
    )
    nodes, feats = mesh.shape["node"], mesh.shape["feat"]

    def per_slice(feature_table, weights, request_rows, *others):
        slots = nodes * request_rows.shape[2]
        plan = per_device
        if feats == 4 and nodes % 2 == 0 and nodes >= 6 and slots % 16 == 0 and slots <= 128 and request_rows.shape[2] <= 8:
            plan = compact_step
        return plan(feature_table, weights, request_rows, *others)

    return jax.shard_map(
        per_slice,
        mesh=mesh,
        in_specs=placed,
        out_specs=(P(("node", "feat"), None), P(None, "feat", None)),
        check_vma=False,
    )
```
